32 devices in a mesh: blk: 16 (over z, y, core), rep: 2 (over x).
Axes of the slice: x: 2, y: 2, z: 4, core: 2. Of those that a mesh axis runs over, the one named last changes fastest.
Arguments:
- features: float32 [16384, 128], P('blk'), may hold values from -6 to 6
- factors: float32 [16384, 128], P('blk'), may hold values from -2.4 to 2.4
Outputs:
- grads: float32 [16384, 128], P(('blk', 'rep'))
The draws below stay inside these ranges and needn't reach their ends.
All inputs are finite; a program needn't handle non-finite values.
Results may differ from the reference program's by a relative error of at most 0.00018.
Values sent between devices are 32-bit elements; how exact they have to be, the bound alone decides.
No kernel may reach another device: no remote copies, remote signals or barrier semaphores. Data moves between devices by JAX's collectives and lax.ppermute only.
A program may use at most 128 MiB of HBM per device.

```python
import jax
import jax.numpy as jnp
from jax import lax

D = 128
RANK = 64
P_DEV = 1024
POINTS = 16384
N_BLK = 16


def level_of(key, extent, cuts, low, high):
    level = 1.0
    for position, shards_of in cuts:
        draws = jax.random.uniform(jax.random.fold_in(jax.random.fold_in(key, 6), position), (shards_of,), jnp.float32, low / len(cuts), high / len(cuts))
        level = level * jnp.repeat(jnp.exp(draws), extent[position] // shards_of).reshape((-1,) + (1,) * (len(extent) - 1 - position))
    return level


def noise(stream_key, extent, spread, limit, cuts=(), dtype=jnp.bfloat16):
    entries = jax.random.normal(stream_key, extent, jnp.float32) * spread
    if len(cuts) > 0:
        entries = level_of(stream_key, extent, cuts, -0.22, 0.18) * entries
    return jnp.clip(entries, min=-limit, max=limit).astype(dtype)


def setup_inputs(seed: int = 0) -> dict:
    seeds = jax.random.split(jax.random.key(seed), 3)
    features = noise(seeds[0], (POINTS, D), 1.0, 6.0, ((0, 16),), jnp.float32)
    factors = noise(seeds[1], (POINTS, 2 * RANK), 0.4, 2.4, ((0, 16),), jnp.float32)
    return {"features": features, "factors": factors}


def reference(features, factors):
    hi = lax.Precision.HIGHEST
    width = features.shape[1]
    all_sq = lax.optimization_barrier(jnp.sum(features * features, axis=1))
    rows_f = features.reshape(N_BLK, P_DEV, width)
    rows_c = factors.reshape(N_BLK, P_DEV, 2 * RANK)

    def block_grad(pair):
        own_feat, own_fac = pair
        cross = jnp.dot(own_feat, features.T, precision=hi)
        own_sq = lax.optimization_barrier(jnp.sum(own_feat * own_feat, axis=1))
        sq_dist = own_sq[:, None] + all_sq[None, :] - 2.0 * cross
        kernel = jnp.exp(-sq_dist / (2.0 * width))
        coupling = jnp.dot(own_fac[:, :RANK], factors[:, RANK:].T, precision=hi)
        coupling = coupling + jnp.dot(own_fac[:, RANK:], factors[:, :RANK].T, precision=hi)
        weight = coupling * kernel
        total = lax.optimization_barrier(jnp.sum(weight, axis=1))[:, None] * own_feat - jnp.dot(weight, features, precision=hi)
        return -total / width
    out = lax.map(block_grad, (rows_f, rows_c))
    return out.reshape(N_BLK * P_DEV, width)
```

```python
import functools
import math

import jax
import jax.numpy as jnp
from jax import lax
from jax.experimental import pallas as pl
from jax.experimental.pallas import tpu as pltpu
from jax.sharding import PartitionSpec as P

F32, BF16 = jnp.float32, jnp.bfloat16
NT = (((1,), (1,)), ((), ()))
VMEM_LIMIT = 56 << 20


def split(x):
    high = x.astype(BF16)
    low = (x - high.astype(F32)).astype(BF16)
    return high, low


def scaled(feat, fac):
    width = feat.shape[1]
    feat = feat * math.sqrt(math.log2(math.e) / width)
    norm = jnp.sum(feat * feat, axis=1, keepdims=True)
    return feat, fac * jnp.exp2(-0.5 * norm)


def prep_kernel(rows_ref, feat_ref, fac_ref):
    width = rows_ref.shape[1] // 2
    feat, fac = scaled(rows_ref[:, :width], rows_ref[:, width:])
    for out, x in ((feat_ref, feat), (fac_ref, fac)):
        high, low = split(x)
        out[:, :width] = high
        out[:, width:] = low


def prep(rows):
    count, width = rows.shape
    block = min(512, count)
    spec = pl.BlockSpec((block, width), lambda i: (i, 0))
    return pl.pallas_call(
        prep_kernel,
        grid=(count // block,),
        in_specs=[spec],
        out_specs=[spec, spec],
        out_shape=[jax.ShapeDtypeStruct((count, width), BF16)] * 2,
        compiler_params=pltpu.CompilerParams(vmem_limit_bytes=VMEM_LIMIT),
        name="prep_rows",
    )(rows)


def pair_kernel(n_units, has_acc, *refs):
    feat_ref, fac_ref = refs[:2]
    units = refs[2 : 2 + n_units]
    acc_ref = refs[2 + n_units] if has_acc else None
    out_ref, cross_rhs, coup_rhs, value = refs[2 + n_units + has_acc :]
    width = out_ref.shape[1]
    first = 0
    for unit in units:
        here = pl.ds(first, unit.shape[0])
        feat, fac = scaled(unit[:, :width], unit[:, width:])
        fac = jnp.concatenate([fac[:, width // 2 :], fac[:, : width // 2]], axis=1)
        high, low = split(feat)
        cross_rhs[here, :] = jnp.concatenate([high, high, low, low], axis=1)
        value[here, :] = jnp.concatenate([high, low], axis=1)
        high, low = split(fac)
        coup_rhs[here, :] = jnp.concatenate([high, high, low, low], axis=1)
        first += unit.shape[0]
    count = first
    tile = math.gcd(256, count)
    rows = math.gcd(1024, out_ref.shape[0])

    def dot_nt(a, b):
        return lax.dot_general(a, b, NT, preferred_element_type=F32)

    def chunk(i, _):
        at = pl.ds(pl.multiple_of(i * rows, rows), rows)
        feat, fac = feat_ref[at, :], fac_ref[at, :]
        total, sums_high, sums_low = None, None, None
        for j in range(0, count, tile):
            here = slice(j, j + tile)
            cross = dot_nt(feat, cross_rhs[here, : 2 * width]) + dot_nt(feat, cross_rhs[here, 2 * width :])
            coup = dot_nt(fac, coup_rhs[here, : 2 * width]) + dot_nt(fac, coup_rhs[here, 2 * width :])
            weight = jnp.exp2(cross) * coup
            high = weight.astype(BF16)
            back = high.astype(F32)
            rest = weight - back
            low = rest.astype(BF16)
            both = jnp.dot(high, value[here, :], preferred_element_type=F32)
            one = jnp.dot(low, value[here, :width], preferred_element_type=F32)
            term = both[:, :width] + both[:, width:] + one
            total = term if total is None else total + term
            for k in range(0, tile, width):
                sums_high = back[:, k : k + width] if sums_high is None else sums_high + back[:, k : k + width]
                rest32 = low.astype(F32)[:, k : k + width]
                sums_low = rest32 if sums_low is None else sums_low + rest32
        sum_high = jnp.sum(sums_high, axis=1, keepdims=True)
        sum_low = jnp.sum(sums_low, axis=1, keepdims=True)
        own_high, own_low = feat[:, :width].astype(F32), feat[:, width:].astype(F32)
        term = total - sum_high * (own_high + own_low) - sum_low * own_high
        out_ref[at, :] = term if acc_ref is None else acc_ref[at, :] + term
        return 0

    lax.fori_loop(0, out_ref.shape[0] // rows, chunk, 0)


def pairs(feat, fac, units, acc=None, start=0, rows=None):
    width = feat.shape[1] // 2
    rows = feat.shape[0] if rows is None else rows
    count = sum(u.shape[0] for u in units)
    block = start // rows
    row_spec = pl.BlockSpec((rows, 2 * width), lambda i: (block, 0))
    acc_spec = pl.BlockSpec((rows, width), lambda i: (block, 0))
    unit_specs = [pl.BlockSpec(u.shape, lambda i: (0, 0)) for u in units]
    has_acc = acc is not None
    whole = rows == feat.shape[0]
    n_pairs = rows * count
    return pl.pallas_call(
        functools.partial(pair_kernel, len(units), has_acc),
        grid=(1,),
        in_specs=[row_spec, row_spec, *unit_specs] + [acc_spec] * has_acc,
        out_specs=pl.BlockSpec((rows, width), lambda i: (0, 0)),
        out_shape=jax.ShapeDtypeStruct((rows, width), F32),
        scratch_shapes=[
            pltpu.VMEM((count, 4 * width), BF16),
            pltpu.VMEM((count, 4 * width), BF16),
            pltpu.VMEM((count, 2 * width), BF16),
        ],
        input_output_aliases={2 + len(units): 0} if has_acc and whole else {},
        compiler_params=pltpu.CompilerParams(vmem_limit_bytes=VMEM_LIMIT),
        cost_estimate=pl.CostEstimate(
            flops=2 * n_pairs * 12 * width, bytes_accessed=8 * rows * width + 8 * count * width, transcendentals=n_pairs
        ),
        name="pair_terms",
    )(feat, fac, *units, *([acc] if has_acc else []))


def ring_order(homes):
    if homes % 2:
        return list(range(homes))
    return list(range(0, homes, 2)) + list(range(homes - 1, 0, -2))


def body(features, factors):
    count, width = features.shape
    replicas = lax.axis_size("rep")
    blocks = lax.axis_size("blk")
    cores = 2 if blocks % 2 == 0 else 1
    homes = blocks // cores
    share = count // replicas
    rep = lax.axis_index("rep")
    order = ring_order(homes)

    def ring(x, by):
        moves = [
            (order[p] * cores + c, order[(p + by) % homes] * cores + c) for p in range(homes) for c in range(cores)
        ]
        return lax.ppermute(x, "blk", moves)

    def other_core(x):
        return lax.ppermute(x, "blk", [(b, b ^ 1) for b in range(blocks)])

    own = jnp.concatenate([features, factors], axis=1)
    own = lax.dynamic_slice_in_dim(jnp.concatenate([own, own]), (rep + 1) % replicas * share, count, 0)
    unit = own[count - share :]

    full = (homes - 1) // 2
    ahead, behind = [unit], [unit]
    for _ in range(full):
        ahead.append(ring(ahead[-1], 1))
        behind.append(ring(behind[-1], -1))
    last = ahead[full:] + behind[full:] if full else []
    if homes % 2 == 0 and homes > 1:
        last = [ring(ahead[full][: share // 2], 1), ring(behind[full][share // 2 :], -1)]
        steps = [[unit]] + [[ahead[s], behind[s]] for s in range(1, full + 1)]
    else:
        steps = [[unit]] + [[ahead[s], behind[s]] for s in range(1, full)]
        if not last:
            steps, last = [], [unit]

    rows = jnp.concatenate([other_core(own), own]) if cores == 2 else own
    feat, fac = prep(rows)
    acc = None
    for units in steps:
        acc = pairs(feat, fac, units, acc)
    if acc is None:
        acc = jnp.zeros((rows.shape[0], width), F32)

    at = 0
    carried = None
    if cores == 2:
        carried = other_core(pairs(feat, fac, last, acc, 0, count))
        at = count
    mine = None
    arrived = []
    for k in range(1, replicas):
        part = pairs(feat, fac, last, acc, at, share)
        if carried is not None:
            part = part + carried[(k - 1) * share : k * share]
        arrived.append(lax.ppermute(part, "rep", [(r, (r + k) % replicas) for r in range(replicas)]))
        at += share
    mine = pairs(feat, fac, last, acc, at, share)
    if carried is not None:
        mine = mine + carried[count - share :]
    for part in arrived:
        mine = mine + part
    return mine * (1.0 / (width * math.sqrt(math.log2(math.e) / width)))


def solution(mesh):
    placed = (P("blk", None), P("blk", None))
    return jax.shard_map(
        body, mesh=mesh, in_specs=placed, out_specs=P(("blk", "rep"), None), check_vma=False
    )
```

```python
import functools
import math

import jax
import jax.numpy as jnp
from jax import lax
from jax.experimental import pallas as pl
from jax.experimental.pallas import tpu as pltpu
from jax.sharding import PartitionSpec as P

F32, BF16 = jnp.float32, jnp.bfloat16
NT = (((1,), (1,)), ((), ()))
VMEM_LIMIT = 16 << 20
IN_VMEM = pl.BlockSpec(memory_space=pltpu.VMEM)


def split(x):
    high = x.astype(BF16)
    low = (x - high.astype(F32)).astype(BF16)
    return high, low


def call(kernel, name, out, *args, scratch=(), pairs=0, aliases=None):
    width = 128
    return pl.pallas_call(
        kernel,
        in_specs=[IN_VMEM] * len(args),
        out_specs=jax.tree.map(lambda _: IN_VMEM, out),
        out_shape=out,
        scratch_shapes=scratch,
        input_output_aliases=aliases or {},
        compiler_params=pltpu.CompilerParams(vmem_limit_bytes=VMEM_LIMIT),
        cost_estimate=pl.CostEstimate(flops=2 * pairs * 12 * width, bytes_accessed=4 << 20, transcendentals=pairs),
        name=name,
    )(*args)


def scale_kernel(feat_ref, fac_ref, out_ref):
    width = feat_ref.shape[1]
    feat = feat_ref[...] * math.sqrt(math.log2(math.e) / width)
    norm = jnp.sum(feat * feat, axis=1, keepdims=True)
    out_ref[:, :width] = feat
    out_ref[:, width:] = fac_ref[...] * jnp.exp2(-0.5 * norm)


def split_kernel(rows_ref, feat_ref, fac_ref):
    width = rows_ref.shape[1] // 2
    for out, at in ((feat_ref, 0), (fac_ref, width)):
        high, low = split(rows_ref[:, at : at + width])
        out[:, :width] = high
        out[:, width:] = low


def split_rows(rows):
    shape = jax.ShapeDtypeStruct(rows.shape, BF16)
    return call(split_kernel, "split_rows", (shape, shape), rows)


def pair_kernel(n_units, has_acc, start, *refs):
    feat_ref, fac_ref = refs[:2]
    units = refs[2 : 2 + n_units]
    acc_ref = refs[2 + n_units] if has_acc else None
    out_ref, cross_rhs, coup_rhs, value = refs[2 + n_units + has_acc :]
    width = out_ref.shape[1]
    first = 0
    for unit in units:
        here = pl.ds(first, unit.shape[0])
        high, low = split(unit[:, :width])
        cross_rhs[here, :] = jnp.concatenate([high, high, low, low], axis=1)
        value[here, :] = jnp.concatenate([high, low, high, jnp.ones_like(high)], axis=1)
        fac = unit[:, width:]
        high, low = split(jnp.concatenate([fac[:, width // 2 :], fac[:, : width // 2]], axis=1))
        coup_rhs[here, :] = jnp.concatenate([high, high, low, low], axis=1)
        first += unit.shape[0]
    count = first
    tile = math.gcd(256, count)
    rows = math.gcd(1024, out_ref.shape[0])

    def dot_nt(a, b):
        return lax.dot_general(a, b, NT, preferred_element_type=F32)

    def chunk(i, _):
        at = pl.ds(pl.multiple_of(i * rows, rows), rows)
        own = pl.ds(pl.multiple_of(start + i * rows, math.gcd(start, rows)), rows)
        feat, fac = feat_ref[own, :], fac_ref[own, :]
        high_sum, low_sum, sums = None, None, None
        for j in range(0, count, tile):
            here = slice(j, j + tile)
            cross = dot_nt(feat, cross_rhs[here, : 2 * width]) + dot_nt(feat, cross_rhs[here, 2 * width :])
            coup = dot_nt(fac, coup_rhs[here, : 2 * width]) + dot_nt(fac, coup_rhs[here, 2 * width :])
            weight = jnp.exp2(cross) * coup
            high = weight.astype(BF16)
            back = high.astype(F32)
            low = (weight - back).astype(BF16)
            a = jnp.dot(high, value[here, : 2 * width], preferred_element_type=F32)
            b = jnp.dot(low, value[here, 2 * width :], preferred_element_type=F32)
            high_sum = a if high_sum is None else high_sum + a
            low_sum = b if low_sum is None else low_sum + b
            for k in range(0, tile, width):
                sums = back[:, k : k + width] if sums is None else sums + back[:, k : k + width]
        total = high_sum[:, :width] + high_sum[:, width:] + low_sum[:, :width]
        own_high, own_low = feat[:, :width].astype(F32), feat[:, width:].astype(F32)
        total = total - jnp.sum(sums, axis=1, keepdims=True) * (own_high + own_low) - low_sum[:, width:] * own_high
        out_ref[at, :] = total if acc_ref is None else acc_ref[at, :] + total
        return 0

    lax.fori_loop(0, out_ref.shape[0] // rows, chunk, 0)


def pairs(feat, fac, units, acc=None, start=0, rows=None):
    width = feat.shape[1] // 2
    rows = feat.shape[0] if rows is None else rows
    count = sum(u.shape[0] for u in units)
    has_acc = acc is not None
    return call(
        functools.partial(pair_kernel, len(units), has_acc, start),
        "pair_terms",
        jax.ShapeDtypeStruct((rows, width), F32),
        feat,
        fac,
        *units,
        *([acc] if has_acc else []),
        scratch=[pltpu.VMEM((count, 4 * width), BF16)] * 3,
        pairs=rows * count,
        aliases={2 + len(units): 0} if has_acc else None,
    )


def ring_order(homes):
    if homes % 2:
        return list(range(homes))
    return list(range(0, homes, 2)) + list(range(homes - 1, 0, -2))


def body(features, factors):
    count, width = features.shape
    replicas = lax.axis_size("rep")
    blocks = lax.axis_size("blk")
    cores = 2 if blocks % 2 == 0 else 1
    homes = blocks // cores
    share = count // replicas
    rep = lax.axis_index("rep")
    order = ring_order(homes)
    after = lax.optimization_barrier

    def ring(x, by):
        moves = [
            (order[p] * cores + c, order[(p + by) % homes] * cores + c) for p in range(homes) for c in range(cores)
        ]
        return lax.ppermute(x, "blk", moves)

    def other_core(x):
        return lax.ppermute(x, "blk", [(b, b ^ 1) for b in range(blocks)])

    own = call(scale_kernel, "scale", jax.ShapeDtypeStruct((count, 2 * width), F32), features, factors)
    unit = lax.dynamic_slice_in_dim(own, rep * share, share, 0)
    full = (homes - 1) // 2
    halves = homes % 2 == 0 and homes > 1
    rows = lax.dynamic_slice_in_dim(jnp.concatenate([own, own]), (rep + 1) % replicas * share, count, 0)

    ahead = behind = unit
    if homes > 1:
        ahead, behind = ring(unit, 1), ring(unit, -1)
    if cores == 2:
        rows = jnp.concatenate([other_core(rows), rows])
    feat, fac = split_rows(rows)
    acc = pairs(feat, fac, [unit])
    last = []
    for step in range(1, full + 1):
        ahead, behind, acc = after((ahead, behind, acc))
        now = [ahead, behind]
        if step < full:
            ahead, behind = ring(ahead, 1), ring(behind, -1)
        elif halves:
            last = [ring(ahead[: share // 2], 1), ring(behind[share // 2 :], -1)]
        acc = pairs(feat, fac, now, acc)
    if halves and not last:
        last = [ahead[: share // 2], behind[share // 2 :]]
    if last:
        *last, acc = after((*last, acc))

    def finish(start, size):
        part = acc[start : start + size]
        return pairs(feat, fac, last, part, start, size) if last else part

    at = 0
    carried = None
    if cores == 2:
        carried = other_core(finish(0, count))
        at = count
    arrived = []
    for k in range(1, replicas):
        part = finish(at, share)
        if carried is not None:
            part = part + carried[(k - 1) * share : k * share]
        arrived.append(lax.ppermute(part, "rep", [(r, (r + k) % replicas) for r in range(replicas)]))
        at += share
    mine = finish(at, share)
    if carried is not None:
        mine = mine + carried[count - share :]
    for part in arrived:
        mine = mine + part
    return mine * (1.0 / (width * math.sqrt(math.log2(math.e) / width)))


def solution(mesh):
    placed = (P("blk", None), P("blk", None))
    return jax.shard_map(
        body, mesh=mesh, in_specs=placed, out_specs=P(("blk", "rep"), None), check_vma=False
    )
```

```python
import functools
import math

import jax
import jax.numpy as jnp
from jax import lax
from jax.experimental import pallas as pl
from jax.experimental.pallas import tpu as pltpu
from jax.sharding import PartitionSpec as P

F32, BF16 = jnp.float32, jnp.bfloat16
NT = (((1,), (1,)), ((), ()))
VMEM_LIMIT = 16 << 20
IN_VMEM = pl.BlockSpec(memory_space=pltpu.VMEM)


def split(x):
    high = x.astype(BF16)
    low = (x - high.astype(F32)).astype(BF16)
    return high, low


def call(kernel, name, out, *args, scratch=(), pairs=0, aliases=None):
    width = 128
    return pl.pallas_call(
        kernel,
        in_specs=[IN_VMEM] * len(args),
        out_specs=jax.tree.map(lambda _: IN_VMEM, out),
        out_shape=out,
        scratch_shapes=scratch,
        input_output_aliases=aliases or {},
        compiler_params=pltpu.CompilerParams(vmem_limit_bytes=VMEM_LIMIT),
        cost_estimate=pl.CostEstimate(flops=2 * pairs * 12 * width, bytes_accessed=4 << 20, transcendentals=pairs),
        name=name,
    )(*args)


def scale(feat, fac):
    width = feat.shape[1]
    feat = feat * math.sqrt(math.log2(math.e) / width)
    norm = jnp.sum(feat * feat, axis=1, keepdims=True)
    return feat, fac * jnp.exp2(-0.5 * norm)


def unit_kernel(rep_ref, feat_hbm, fac_hbm, *refs):
    outs, (feat_ref, fac_ref, sem) = refs[:-3], refs[-3:]
    share, width = feat_ref.shape
    here = pl.ds(pl.multiple_of(rep_ref[0] * share, share), share)
    copies = [
        pltpu.make_async_copy(src.at[here, :], dst, sem.at[k])
        for k, (src, dst) in enumerate(((feat_hbm, feat_ref), (fac_hbm, fac_ref)))
    ]
    for copy in copies:
        copy.start()
    for copy in copies:
        copy.wait()
    part = share // len(outs)
    for k, out in enumerate(outs):
        feat, fac = scale(feat_ref[k * part : (k + 1) * part, :], fac_ref[k * part : (k + 1) * part, :])
        out[:, :width] = feat
        out[:, width:] = fac


def own_units(rep, features, factors, share, parts):
    width = features.shape[1]
    out = jax.ShapeDtypeStruct((share // parts, 2 * width), F32)
    return pl.pallas_call(
        unit_kernel,
        in_specs=[pl.BlockSpec(memory_space=pltpu.SMEM)] + [pl.BlockSpec(memory_space=pltpu.HBM)] * 2,
        out_specs=[IN_VMEM] * parts,
        out_shape=[out] * parts,
        scratch_shapes=[pltpu.VMEM((share, width), F32)] * 2 + [pltpu.SemaphoreType.DMA((2,))],
        compiler_params=pltpu.CompilerParams(vmem_limit_bytes=VMEM_LIMIT),
        name="own_units",
    )(rep, features, factors)


def rows_kernel(replicas, rep_ref, *refs):
    sources, (feat_out, fac_out) = refs[:-2], refs[-2:]
    count, width = sources[0].shape
    share = count // replicas
    for block in range(len(sources) // 2):
        feat_ref, fac_ref = sources[2 * block : 2 * block + 2]
        for k in range(replicas):
            place = lax.rem(k - rep_ref[0] - 1 + replicas, replicas) * share + block * count
            at = pl.ds(pl.multiple_of(place, share), share)
            here = slice(k * share, (k + 1) * share)
            for out, x in zip((feat_out, fac_out), scale(feat_ref[here, :], fac_ref[here, :]), strict=True):
                high, low = split(x)
                out[at, :width] = high
                out[at, width:] = low


def split_rows(rep, replicas, *blocks):
    count, width = blocks[0].shape
    out = jax.ShapeDtypeStruct((count * len(blocks) // 2, 2 * width), BF16)
    return pl.pallas_call(
        functools.partial(rows_kernel, replicas),
        in_specs=[pl.BlockSpec(memory_space=pltpu.SMEM)] + [IN_VMEM] * len(blocks),
        out_specs=[IN_VMEM] * 2,
        out_shape=[out] * 2,
        compiler_params=pltpu.CompilerParams(vmem_limit_bytes=VMEM_LIMIT),
        name="split_rows",
    )(rep, *blocks)


def pair_kernel(n_units, has_acc, start, *refs):
    feat_ref, fac_ref = refs[:2]
    units = refs[2 : 2 + n_units]
    acc_ref = refs[2 + n_units] if has_acc else None
    out_ref, cross_rhs, coup_rhs, value = refs[2 + n_units + has_acc :]
    width = out_ref.shape[1]
    first = 0
    for unit in units:
        here = pl.ds(first, unit.shape[0])
        high, low = split(unit[:, :width])
        cross_rhs[here, :] = jnp.concatenate([high, high, low, low], axis=1)
        value[here, :] = jnp.concatenate([high, low, high, jnp.ones_like(high)], axis=1)
        fac = unit[:, width:]
        high, low = split(jnp.concatenate([fac[:, width // 2 :], fac[:, : width // 2]], axis=1))
        coup_rhs[here, :] = jnp.concatenate([high, high, low, low], axis=1)
        first += unit.shape[0]
    count = first
    tile = math.gcd(256, count)
    rows = math.gcd(1024, out_ref.shape[0])

    def dot_nt(a, b):
        return lax.dot_general(a, b, NT, preferred_element_type=F32)

    def chunk(i, _):
        at = pl.ds(pl.multiple_of(i * rows, rows), rows)
        own = pl.ds(pl.multiple_of(start + i * rows, math.gcd(start, rows)), rows)
        feat, fac = feat_ref[own, :], fac_ref[own, :]
        high_sum, low_sum, sums = None, None, None
        for j in range(0, count, tile):
            here = slice(j, j + tile)
            cross = dot_nt(feat, cross_rhs[here, : 2 * width]) + dot_nt(feat, cross_rhs[here, 2 * width :])
            coup = dot_nt(fac, coup_rhs[here, : 2 * width]) + dot_nt(fac, coup_rhs[here, 2 * width :])
            weight = jnp.exp2(cross) * coup
            high = weight.astype(BF16)
            back = high.astype(F32)
            low = (weight - back).astype(BF16)
            a = jnp.dot(high, value[here, : 2 * width], preferred_element_type=F32)
            b = jnp.dot(low, value[here, 2 * width :], preferred_element_type=F32)
            high_sum = a if high_sum is None else high_sum + a
            low_sum = b if low_sum is None else low_sum + b
            for k in range(0, tile, width):
                sums = back[:, k : k + width] if sums is None else sums + back[:, k : k + width]
        total = high_sum[:, :width] + high_sum[:, width:] + low_sum[:, :width]
        own_high, own_low = feat[:, :width].astype(F32), feat[:, width:].astype(F32)
        total = total - jnp.sum(sums, axis=1, keepdims=True) * (own_high + own_low) - low_sum[:, width:] * own_high
        out_ref[at, :] = total if acc_ref is None else acc_ref[own, :] + total
        return 0

    lax.fori_loop(0, out_ref.shape[0] // rows, chunk, 0)


def pairs(feat, fac, units, acc=None, start=0, rows=None):
    width = feat.shape[1] // 2
    rows = feat.shape[0] if rows is None else rows
    count = sum(u.shape[0] for u in units)
    has_acc = acc is not None
    return call(
        functools.partial(pair_kernel, len(units), has_acc, start),
        "pair_terms",
        jax.ShapeDtypeStruct((rows, width), F32),
        feat,
        fac,
        *units,
        *([acc] if has_acc else []),
        scratch=[pltpu.VMEM((count, 4 * width), BF16)] * 3,
        pairs=rows * count,
        aliases={2 + len(units): 0} if has_acc and rows == feat.shape[0] else None,
    )


def ring_order(homes):
    if homes % 2:
        return list(range(homes))
    return list(range(0, homes, 2)) + list(range(homes - 1, 0, -2))


def body(features, factors):
    count, width = features.shape
    replicas = lax.axis_size("rep")
    blocks = lax.axis_size("blk")
    cores = 2 if blocks % 2 == 0 else 1
    homes = blocks // cores
    share = count // replicas
    rep = lax.axis_index("rep")
    order = ring_order(homes)
    after = lax.optimization_barrier

    def ring(x, by):
        moves = [
            (order[p] * cores + c, order[(p + by) % homes] * cores + c) for p in range(homes) for c in range(cores)
        ]
        return lax.ppermute(x, "blk", moves)

    def other_core(x):
        return lax.ppermute(x, "blk", [(b, b ^ 1) for b in range(blocks)])

    rep_ref = rep.astype(jnp.int32).reshape(1)
    parts = 2 if share % 32 == 0 else 1
    full = (homes - 1) // 2
    halves = homes % 2 == 0 and homes > 1

    ahead = list(own_units(rep_ref, features, factors, share, parts))
    behind = list(ahead)
    own = list(ahead)
    if homes > 1:
        for p in range(parts):
            ahead[p], behind[p] = ring(ahead[p], 1), ring(behind[p], -1)
    if cores == 2:
        feat, fac = split_rows(rep_ref, replicas, other_core(features), other_core(factors), features, factors)
    else:
        feat, fac = split_rows(rep_ref, replicas, features, factors)
    acc = pairs(feat, fac, own)
    last = []
    for step in range(1, full + 1):
        for p in range(parts):
            ahead[p], behind[p], acc = after((ahead[p], behind[p], acc))
            now = [ahead[p], behind[p]]
            if step < full:
                ahead[p], behind[p] = ring(ahead[p], 1), ring(behind[p], -1)
            elif halves and parts == 2:
                last.append(ring(ahead[p], 1) if p == 0 else ring(behind[p], -1))
            elif halves:
                last = [ring(ahead[p][: share // 2], 1), ring(behind[p][share // 2 :], -1)]
            acc = pairs(feat, fac, now, acc)
    if halves and not full:
        last = [ahead[0], behind[1]] if parts == 2 else [ahead[0][: share // 2], behind[0][share // 2 :]]
    if last:
        *last, acc = after((*last, acc))

    def finish(start, size):
        return pairs(feat, fac, last, acc, start, size) if last else acc[start : start + size]

    base = count if cores == 2 else 0
    arrived = []
    for k in range(replicas):
        at = k * share
        theirs = other_core(finish(at, share)) if cores == 2 else None
        mine = finish(base + at, share)
        if cores == 2:
            mine = mine + theirs
        if k < replicas - 1:
            arrived.append(lax.ppermute(mine, "rep", [(r, (r + k + 1) % replicas) for r in range(replicas)]))
    for part in arrived:
        mine = mine + part
    return mine * (1.0 / (width * math.sqrt(math.log2(math.e) / width)))


def solution(mesh):
    placed = (P("blk", None), P("blk", None))
    return jax.shard_map(
        body, mesh=mesh, in_specs=placed, out_specs=P(("blk", "rep"), None), check_vma=False
    )
```

```python
import functools
import math

import jax
import jax.numpy as jnp
from jax import lax
from jax.experimental import pallas as pl
from jax.experimental.pallas import tpu as pltpu
from jax.sharding import PartitionSpec as P

F32, BF16 = jnp.float32, jnp.bfloat16
NT = (((1,), (1,)), ((), ()))
VMEM_LIMIT = 16 << 20
IN_VMEM = pl.BlockSpec(memory_space=pltpu.VMEM)


def split(x):
    high = x.astype(BF16)
    low = (x - high.astype(F32)).astype(BF16)
    return high, low


def call(kernel, name, out, *args, scratch=(), pairs=0, aliases=None):
    width = 128
    return pl.pallas_call(
        kernel,
        in_specs=[IN_VMEM] * len(args),
        out_specs=jax.tree.map(lambda _: IN_VMEM, out),
        out_shape=out,
        scratch_shapes=scratch,
        input_output_aliases=aliases or {},
        compiler_params=pltpu.CompilerParams(vmem_limit_bytes=VMEM_LIMIT),
        cost_estimate=pl.CostEstimate(flops=2 * pairs * 12 * width, bytes_accessed=4 << 20, transcendentals=pairs),
        name=name,
    )(*args)


def scale(feat, fac):
    width = feat.shape[1]
    feat = feat * math.sqrt(math.log2(math.e) / width)
    norm = jnp.sum(feat * feat, axis=1, keepdims=True)
    return feat, fac * jnp.exp2(-0.5 * norm)


def rows_kernel(replicas, blocks, block, rep_ref, feat_ref, fac_ref, *refs):
    feat_out, fac_out = refs[-2:]
    count, width = feat_ref.shape
    share = count // replicas
    for k in range(replicas):
        place = lax.rem(k - rep_ref[0] - 1 + replicas, replicas) * (blocks * share) + block * share
        at = pl.ds(pl.multiple_of(place, share), share)
        here = slice(k * share, (k + 1) * share)
        for out, x in zip((feat_out, fac_out), scale(feat_ref[here, :], fac_ref[here, :]), strict=True):
            high, low = split(x)
            out[at, :width] = high
            out[at, width:] = low


def split_rows(rep, replicas, blocks, block, feat, fac, filled=()):
    count, width = feat.shape
    out = jax.ShapeDtypeStruct((count * blocks, 2 * width), BF16)
    return pl.pallas_call(
        functools.partial(rows_kernel, replicas, blocks, block),
        in_specs=[pl.BlockSpec(memory_space=pltpu.SMEM)] + [IN_VMEM] * (2 + len(filled)),
        out_specs=[IN_VMEM] * 2,
        out_shape=[out] * 2,
        input_output_aliases={3: 0, 4: 1} if filled else {},
        compiler_params=pltpu.CompilerParams(vmem_limit_bytes=VMEM_LIMIT),
        name="split_rows",
    )(rep, feat, fac, *filled)


def pair_kernel(n_units, has_acc, start, acc_start, size, *refs):
    feat_ref, fac_ref = refs[:2]
    units = refs[2 : 2 + n_units]
    acc_ref = refs[2 + n_units] if has_acc else None
    out_ref, cross_rhs, coup_rhs, value = refs[2 + n_units + has_acc :]
    width = out_ref.shape[1]
    first = 0
    for unit in units:
        here = pl.ds(first, unit.shape[0])
        high, low = split(unit[:, :width])
        cross_rhs[here, :] = jnp.concatenate([high, high, low, low], axis=1)
        value[here, :] = jnp.concatenate([high, low, high, jnp.ones_like(high)], axis=1)
        fac = unit[:, width:]
        high, low = split(jnp.concatenate([fac[:, width // 2 :], fac[:, : width // 2]], axis=1))
        coup_rhs[here, :] = jnp.concatenate([high, high, low, low], axis=1)
        first += unit.shape[0]
    count = first
    tile = math.gcd(256, count)
    rows = math.gcd(1024, size)

    def dot_nt(a, b):
        return lax.dot_general(a, b, NT, preferred_element_type=F32)

    def chunk(i, _):
        at = pl.ds(pl.multiple_of(i * rows, rows), rows)
        own = pl.ds(pl.multiple_of(start + i * rows, math.gcd(start, rows)), rows)
        before = pl.ds(pl.multiple_of(acc_start + i * rows, math.gcd(acc_start, rows)), rows)
        feat, fac = feat_ref[own, :], fac_ref[own, :]
        high_sum, low_sum, sums = None, None, None
        for j in range(0, count, tile):
            here = slice(j, j + tile)
            cross = dot_nt(feat, cross_rhs[here, : 2 * width]) + dot_nt(feat, cross_rhs[here, 2 * width :])
            coup = dot_nt(fac, coup_rhs[here, : 2 * width]) + dot_nt(fac, coup_rhs[here, 2 * width :])
            weight = jnp.exp2(cross) * coup
            high = weight.astype(BF16)
            back = high.astype(F32)
            low = (weight - back).astype(BF16)
            a = jnp.dot(high, value[here, : 2 * width], preferred_element_type=F32)
            b = jnp.dot(low, value[here, 2 * width :], preferred_element_type=F32)
            high_sum = a if high_sum is None else high_sum + a
            low_sum = b if low_sum is None else low_sum + b
            for k in range(0, tile, width):
                sums = back[:, k : k + width] if sums is None else sums + back[:, k : k + width]
        total = high_sum[:, :width] + high_sum[:, width:] + low_sum[:, :width]
        own_high, own_low = feat[:, :width].astype(F32), feat[:, width:].astype(F32)
        total = total - jnp.sum(sums, axis=1, keepdims=True) * (own_high + own_low) - low_sum[:, width:] * own_high
        out_ref[at, :] = total if acc_ref is None else acc_ref[before, :] + total
        return 0

    lax.fori_loop(0, size // rows, chunk, 0)
    if size < out_ref.shape[0]:
        out_ref[size:, :] = jnp.zeros_like(out_ref[size:, :])


def pairs(feat, fac, units, acc=None, start=0, rows=None, acc_start=0, size=None):
    width = feat.shape[1] // 2
    rows = feat.shape[0] if rows is None else rows
    size = rows if size is None else size
    count = sum(u.shape[0] for u in units)
    has_acc = acc is not None
    return call(
        functools.partial(pair_kernel, len(units), has_acc, start, start - acc_start, size),
        "pair_terms",
        jax.ShapeDtypeStruct((rows, width), F32),
        feat,
        fac,
        *units,
        *([acc] if has_acc else []),
        scratch=[pltpu.VMEM((count, 4 * width), BF16)] * 3,
        pairs=size * count,
        aliases={2 + len(units): 0} if has_acc and rows == acc.shape[0] else None,
    )


def ring_order(homes):
    if homes % 2:
        return list(range(homes))
    return list(range(0, homes, 2)) + list(range(homes - 1, 0, -2))


def body(features, factors):
    replicas = lax.axis_size("rep")
    blocks = lax.axis_size("blk")
    count, width = features.shape
    share = count // replicas
    rep = lax.axis_index("rep")
    rep_ref = rep.astype(jnp.int32).reshape(1)
    homes = blocks // 2
    order = ring_order(homes)
    after = lax.optimization_barrier

    def ring(x):
        moves = []
        for p in range(homes):
            moves += [(order[p] * 2 + c, order[(p + 1 - 2 * c) % homes] * 2 + c) for c in range(2)]
        return lax.ppermute(x, "blk", moves)

    def other_core(x):
        return lax.ppermute(x, "blk", [(b, b ^ 1) for b in range(blocks)])

    def units_of(*blocks):
        return jnp.concatenate(scale(*(lax.dynamic_slice_in_dim(x, rep * share, share) for x in blocks)), axis=1)

    own = units_of(features, factors)
    first = ring(own)
    own, features, factors = after((own, features, factors))
    filled = split_rows(rep_ref, replicas, 2, 1, features, factors)
    *filled, features, factors = after((*filled, features, factors))
    features, factors = other_core(features), other_core(factors)
    second = ring(units_of(features, factors))
    feat, fac = split_rows(rep_ref, replicas, 2, 0, features, factors, filled)
    mine_at = 2 * share * (replicas - 1)
    acc = pairs(feat, fac, [own], size=mine_at) if mine_at else jnp.zeros((2 * count, width), F32)

    full = (homes - 1) // 2
    total = 2 * full + (homes + 1) % 2
    flying = [first, second]
    for step in range(total - 1):
        here, acc = after((flying[step % 2], acc))
        if step + 2 < total:
            flying[step % 2] = ring(here)
        acc = pairs(feat, fac, [here], acc)
    last, acc = after((flying[(total - 1) % 2], acc))

    arrived = []
    for k in range(replicas - 1):
        at = k * 2 * share
        received = other_core(pairs(feat, fac, [last], acc, at, share))
        part = pairs(feat, fac, [last], acc, at + share, share) + received
        arrived.append(lax.ppermute(part, "rep", [(r, (r + k + 1) % replicas) for r in range(replicas)]))
        acc, part = after((acc, part))
    part = pairs(feat, fac, [own, last], acc, mine_at, 2 * share)
    part = part[share:] + other_core(part[:share])
    for x in arrived:
        part = part + x
    return part * (1.0 / (width * math.sqrt(math.log2(math.e) / width)))


def solution(mesh):
    placed = (P("blk", None), P("blk", None))
    return jax.shard_map(
        body, mesh=mesh, in_specs=placed, out_specs=P(("blk", "rep"), None), check_vma=False
    )
```

```python
import functools
import math

import jax
import jax.numpy as jnp
from jax import lax
from jax.experimental import pallas as pl
from jax.experimental.pallas import tpu as pltpu
from jax.sharding import PartitionSpec as P

F32, BF16 = jnp.float32, jnp.bfloat16
NT = (((1,), (1,)), ((), ()))
VMEM_LIMIT = 16 << 20
IN_VMEM = pl.BlockSpec(memory_space=pltpu.VMEM)


def split(x):
    high = x.astype(BF16)
    low = (x - high.astype(F32)).astype(BF16)
    return high, low


def call(kernel, name, out, *args, scratch=(), pairs=0, aliases=None):
    width = 128
    return pl.pallas_call(
        kernel,
        in_specs=[IN_VMEM] * len(args),
        out_specs=jax.tree.map(lambda _: IN_VMEM, out),
        out_shape=out,
        scratch_shapes=scratch,
        input_output_aliases=aliases or {},
        compiler_params=pltpu.CompilerParams(vmem_limit_bytes=VMEM_LIMIT),
        cost_estimate=pl.CostEstimate(flops=2 * pairs * 12 * width, bytes_accessed=4 << 20, transcendentals=pairs),
        name=name,
    )(*args)


def scale(feat, fac):
    width = feat.shape[1]
    feat = feat * math.sqrt(math.log2(math.e) / width)
    norm = jnp.sum(feat * feat, axis=1, keepdims=True)
    return feat, fac * jnp.exp2(-0.5 * norm)


def store_split(out, at, x):
    high, low = split(x)
    out[at, : x.shape[1]] = high
    out[at, x.shape[1] :] = low


def own_rows_kernel(replicas, rep_ref, feat_ref, fac_ref, feat_out, fac_out, *parts):
    count = feat_ref.shape[0]
    share = count // replicas
    for k in range(replicas):
        here = pl.ds(pl.multiple_of(lax.rem(rep_ref[0] + 1 + k, replicas) * share, share), share)
        values = scale(feat_ref[here, :], fac_ref[here, :])
        part, first = divmod(k * share, parts[0].shape[0])
        for out, x, raw in zip((feat_out, fac_out), values, parts[2 * part : 2 * part + 2], strict=True):
            store_split(out, pl.ds((2 * k + 1) * share, share), x)
            raw[first : first + share, :] = x


def own_rows(rep, replicas, feat, fac, part):
    count, width = feat.shape
    split_out = jax.ShapeDtypeStruct((2 * count, 2 * width), BF16)
    outs = [split_out] * 2 + [jax.ShapeDtypeStruct((part, width), F32)] * (2 * (count // part))
    return pl.pallas_call(
        functools.partial(own_rows_kernel, replicas),
        in_specs=[pl.BlockSpec(memory_space=pltpu.SMEM)] + [IN_VMEM] * 2,
        out_specs=[IN_VMEM] * len(outs),
        out_shape=outs,
        compiler_params=pltpu.CompilerParams(vmem_limit_bytes=VMEM_LIMIT),
        name="own_rows",
    )(rep, feat, fac)


def other_rows_kernel(share, n_parts, *refs):
    outs = refs[-2:]
    rows = refs[0].shape[0]
    for part in range(n_parts):
        for first in range(0, rows, share):
            k = (part * rows + first) // share
            for out, x in zip(outs, refs[2 * part : 2 * part + 2], strict=True):
                store_split(out, pl.ds(2 * k * share, share), x[first : first + share, :])


def other_rows(share, parts, filled):
    n_parts = len(parts) // 2
    return pl.pallas_call(
        functools.partial(other_rows_kernel, share, n_parts),
        in_specs=[IN_VMEM] * (len(parts) + 2),
        out_specs=[IN_VMEM] * 2,
        out_shape=[jax.ShapeDtypeStruct(x.shape, x.dtype) for x in filled],
        input_output_aliases={len(parts): 0, len(parts) + 1: 1},
        compiler_params=pltpu.CompilerParams(vmem_limit_bytes=VMEM_LIMIT),
        name="other_rows",
    )(*parts, *filled)


def pair_kernel(n_units, has_acc, start, acc_start, size, *refs):
    feat_ref, fac_ref = refs[:2]
    units = refs[2 : 2 + n_units]
    acc_ref = refs[2 + n_units] if has_acc else None
    out_ref, cross_rhs, coup_rhs, value = refs[2 + n_units + has_acc :]
    width = out_ref.shape[1]
    first = 0
    for unit in units:
        here = pl.ds(first, unit.shape[0])
        high, low = split(unit[:, :width])
        cross_rhs[here, :] = jnp.concatenate([high, high, low, low], axis=1)
        value[here, :] = jnp.concatenate([high, low, high, jnp.ones_like(high)], axis=1)
        fac = unit[:, width:]
        high, low = split(jnp.concatenate([fac[:, width // 2 :], fac[:, : width // 2]], axis=1))
        coup_rhs[here, :] = jnp.concatenate([high, high, low, low], axis=1)
        first += unit.shape[0]
    count = first
    tile = math.gcd(256, count)
    rows = math.gcd(1024, size)

    def dot_nt(a, b):
        return lax.dot_general(a, b, NT, preferred_element_type=F32)

    def chunk(i, _):
        at = pl.ds(pl.multiple_of(i * rows, rows), rows)
        own = pl.ds(pl.multiple_of(start + i * rows, math.gcd(start, rows)), rows)
        before = pl.ds(pl.multiple_of(acc_start + i * rows, math.gcd(acc_start, rows)), rows)
        feat, fac = feat_ref[own, :], fac_ref[own, :]
        high_sum, low_sum, sums = None, None, None
        for j in range(0, count, tile):
            here = slice(j, j + tile)
            cross = dot_nt(feat, cross_rhs[here, : 2 * width]) + dot_nt(feat, cross_rhs[here, 2 * width :])
            coup = dot_nt(fac, coup_rhs[here, : 2 * width]) + dot_nt(fac, coup_rhs[here, 2 * width :])
            weight = jnp.exp2(cross) * coup
            high = weight.astype(BF16)
            back = high.astype(F32)
            low = (weight - back).astype(BF16)
            a = jnp.dot(high, value[here, : 2 * width], preferred_element_type=F32)
            b = jnp.dot(low, value[here, 2 * width :], preferred_element_type=F32)
            high_sum = a if high_sum is None else high_sum + a
            low_sum = b if low_sum is None else low_sum + b
            for k in range(0, tile, width):
                sums = back[:, k : k + width] if sums is None else sums + back[:, k : k + width]
        total = high_sum[:, :width] + high_sum[:, width:] + low_sum[:, :width]
        own_high, own_low = feat[:, :width].astype(F32), feat[:, width:].astype(F32)
        total = total - jnp.sum(sums, axis=1, keepdims=True) * (own_high + own_low) - low_sum[:, width:] * own_high
        out_ref[at, :] = total if acc_ref is None else acc_ref[before, :] + total
        return 0

    lax.fori_loop(0, size // rows, chunk, 0)
    if size < out_ref.shape[0]:
        out_ref[size:, :] = jnp.zeros_like(out_ref[size:, :])


def pairs(feat, fac, units, acc=None, start=0, rows=None, acc_start=0, size=None):
    width = feat.shape[1] // 2
    rows = feat.shape[0] if rows is None else rows
    size = rows if size is None else size
    count = sum(u.shape[0] for u in units)
    has_acc = acc is not None
    return call(
        functools.partial(pair_kernel, len(units), has_acc, start, start - acc_start, size),
        "pair_terms",
        jax.ShapeDtypeStruct((rows, width), F32),
        feat,
        fac,
        *units,
        *([acc] if has_acc else []),
        scratch=[pltpu.VMEM((count, 4 * width), BF16)] * 3,
        pairs=size * count,
        aliases={2 + len(units): 0} if has_acc and rows == acc.shape[0] else None,
    )


def ring_order(homes):
    if homes % 2:
        return list(range(homes))
    return list(range(0, homes, 2)) + list(range(homes - 1, 0, -2))


def body(features, factors):
    replicas = lax.axis_size("rep")
    blocks = lax.axis_size("blk")
    count, width = features.shape
    share = count // replicas
    rep = lax.axis_index("rep")
    rep_ref = rep.astype(jnp.int32).reshape(1)
    homes = blocks // 2
    order = ring_order(homes)
    after = lax.optimization_barrier

    def ring(x):
        moves = []
        for p in range(homes):
            moves += [(order[p] * 2 + c, order[(p + 1 - 2 * c) % homes] * 2 + c) for c in range(2)]
        return lax.ppermute(x, "blk", moves)

    def other_core(x):
        return lax.ppermute(x, "blk", [(b, b ^ 1) for b in range(blocks)])

    slices = (lax.dynamic_slice_in_dim(x, rep * share, share) for x in (features, factors))
    own = jnp.concatenate(scale(*slices), axis=1)
    first = ring(own)
    own, features, factors = after((own, features, factors))
    part = share if replicas <= 4 else count
    made = own_rows(rep_ref, replicas, features, factors, part)
    filled, parts = made[:2], made[2:]
    parts = [other_core(x) for x in parts]
    second = ring(jnp.concatenate([x[part - share :] for x in parts[-2:]], axis=1))
    feat, fac = other_rows(share, parts, filled)
    mine_at = 2 * share * (replicas - 1)

    full = (homes - 1) // 2
    total = 2 * full + (homes + 1) % 2
    flying = [first, second]
    acc = None
    for step in range(total - 1):
        here, feat, fac, acc = after((flying[step % 2], feat, fac, acc))
        if step + 2 < total:
            flying[step % 2] = ring(here)
        if acc is None:
            acc = pairs(feat, fac, [own], size=mine_at)
        acc = pairs(feat, fac, [here], acc)
    last, acc = after((flying[(total - 1) % 2], acc))

    arrived = []
    for k in range(replicas - 1):
        at = k * 2 * share
        received = other_core(pairs(feat, fac, [last], acc, at, share))
        part = pairs(feat, fac, [last], acc, at + share, share) + received
        arrived.append(lax.ppermute(part, "rep", [(r, (r + k + 1) % replicas) for r in range(replicas)]))
        acc, part = after((acc, part))
    part = pairs(feat, fac, [own, last], acc, mine_at, 2 * share)
    half = share // 2
    part = part[share:] + jnp.concatenate([other_core(part[:half]), other_core(part[half:share])])
    for x in arrived:
        part = part + x
    return part * (1.0 / (width * math.sqrt(math.log2(math.e) / width)))


def solution(mesh):
    placed = (P("blk", None), P("blk", None))
    return jax.shard_map(
        body, mesh=mesh, in_specs=placed, out_specs=P(("blk", "rep"), None), check_vma=False
    )
```

```python
import functools
import math

import jax
import jax.numpy as jnp
from jax import lax
from jax.experimental import pallas as pl
from jax.experimental.pallas import tpu as pltpu
from jax.sharding import PartitionSpec as P

F32, BF16 = jnp.float32, jnp.bfloat16
NT = (((1,), (1,)), ((), ()))
VMEM_LIMIT = 16 << 20
IN_VMEM = pl.BlockSpec(memory_space=pltpu.VMEM)


def split(x):
    high = x.astype(BF16)
    low = (x - high.astype(F32)).astype(BF16)
    return high, low


def call(kernel, name, out, *args, scratch=(), pairs=0, aliases=None):
    width = 128
    return pl.pallas_call(
        kernel,
        in_specs=[IN_VMEM] * len(args),
        out_specs=jax.tree.map(lambda _: IN_VMEM, out),
        out_shape=out,
        scratch_shapes=scratch,
        input_output_aliases=aliases or {},
        compiler_params=pltpu.CompilerParams(vmem_limit_bytes=VMEM_LIMIT),
        cost_estimate=pl.CostEstimate(flops=2 * pairs * 12 * width, bytes_accessed=4 << 20, transcendentals=pairs),
        name=name,
    )(*args)


def scale(feat, fac):
    width = feat.shape[1]
    feat = feat * math.sqrt(math.log2(math.e) / width)
    norm = jnp.sum(feat * feat, axis=1, keepdims=True)
    return feat, fac * jnp.exp2(-0.5 * norm)


def store_split(out, at, x):
    parts = split(x)
    for k in range(4):
        out[at, k * x.shape[1] : (k + 1) * x.shape[1]] = parts[k // 2]


def own_rows_kernel(replicas, rep_ref, feat_ref, fac_ref, feat_out, fac_out, *parts):
    count = feat_ref.shape[0]
    share = count // replicas
    for k in range(replicas):
        here = pl.ds(pl.multiple_of(lax.rem(rep_ref[0] + 1 + k, replicas) * share, share), share)
        values = scale(feat_ref[here, :], fac_ref[here, :])
        for x, out, held in zip(values, (feat_out, fac_out), (parts[::2], parts[1::2]), strict=True):
            store_split(out, pl.ds((2 * k + 1) * share, share), x)
            rows = min(share, held[0].shape[0])
            for first in range(0, share, rows):
                part, at = divmod(k * share + first, held[0].shape[0])
                held[part][at : at + rows, :] = x[first : first + rows, :]


def own_rows(rep, replicas, feat, fac, part):
    count, width = feat.shape
    split_out = jax.ShapeDtypeStruct((2 * count, 4 * width), BF16)
    outs = [split_out] * 2 + [jax.ShapeDtypeStruct((part, width), F32)] * (2 * (count // part))
    return pl.pallas_call(
        functools.partial(own_rows_kernel, replicas),
        in_specs=[pl.BlockSpec(memory_space=pltpu.SMEM)] + [IN_VMEM] * 2,
        out_specs=[IN_VMEM] * len(outs),
        out_shape=outs,
        compiler_params=pltpu.CompilerParams(vmem_limit_bytes=VMEM_LIMIT),
        name="own_rows",
    )(rep, feat, fac)


def other_rows_kernel(share, n_parts, *refs):
    outs = refs[-2:]
    held = refs[0].shape[0]
    rows = min(share, held)
    for part in range(n_parts):
        for first in range(0, held, rows):
            k, at = divmod(part * held + first, share)
            for out, x in zip(outs, refs[2 * part : 2 * part + 2], strict=True):
                store_split(out, pl.ds(2 * k * share + at, rows), x[first : first + rows, :])


def other_rows(share, parts, filled):
    n_parts = len(parts) // 2
    return pl.pallas_call(
        functools.partial(other_rows_kernel, share, n_parts),
        in_specs=[IN_VMEM] * (len(parts) + 2),
        out_specs=[IN_VMEM] * 2,
        out_shape=[jax.ShapeDtypeStruct(x.shape, x.dtype) for x in filled],
        input_output_aliases={len(parts): 0, len(parts) + 1: 1},
        compiler_params=pltpu.CompilerParams(vmem_limit_bytes=VMEM_LIMIT),
        name="other_rows",
    )(*parts, *filled)


def pair_kernel(kinds, has_acc, has_more, start, acc_start, *refs):
    feat_ref, fac_ref, *refs = refs
    value, coup_rhs = refs[-2:]
    out_ref = refs[-3]
    more_ref = refs[-4] if has_more else None
    acc_ref = refs[-4 - has_more] if has_acc else None
    width = out_ref.shape[1]
    tiles = []
    for pair in kinds:
        feat, fac, refs = (refs[0], refs[1], refs[2:]) if pair else (refs[0], refs[0], refs[1:])
        tile = math.gcd(256, feat.shape[0])
        tiles += [(feat, fac, at, tile, pair) for at in range(0, feat.shape[0], tile)]
    rows = math.gcd(1024, out_ref.shape[0])

    def dot_nt(a, b):
        return lax.dot_general(a, b, NT, preferred_element_type=F32)

    def place(k):
        first = sum(t[3] for t in tiles[:k])
        return slice(first, first + tiles[k][3])

    def prepare(k):
        feat, fac, at, tile, pair = tiles[k]
        here, at = place(k), slice(at, at + tile)
        high, low = split(feat[at, :width])
        value[here, :] = jnp.concatenate([high, low, high, jnp.ones_like(high)], axis=1)
        fac = fac[at, :] if pair else fac[at, width:]
        high, low = split(jnp.concatenate([fac[:, width // 2 :], fac[:, : width // 2]], axis=1))
        coup_rhs[here, :] = jnp.concatenate([high, low], axis=1)

    def chunk(i, first):
        own = pl.ds(start + i * rows, rows)
        feat, fac = feat_ref[own, :], fac_ref[own, :]
        high_sum, low_sum, sums = None, None, None
        for k in range(len(tiles)):
            if first:
                prepare(k)
            here = place(k)
            both, other = value[here, : 2 * width], coup_rhs[here, :]
            cross = dot_nt(feat[:, : 2 * width], both) + dot_nt(feat[:, 2 * width :], both)
            coup = dot_nt(fac[:, : 2 * width], other) + dot_nt(fac[:, 2 * width :], other)
            weight = jnp.exp2(cross) * coup
            high = weight.astype(BF16)
            back = high.astype(F32)
            low = (weight - back).astype(BF16)
            a = jnp.dot(high, both, preferred_element_type=F32)
            b = jnp.dot(low, value[here, 2 * width :], preferred_element_type=F32)
            high_sum = a if high_sum is None else high_sum + a
            low_sum = b if low_sum is None else low_sum + b
            for k in range(0, weight.shape[1], width):
                sums = back[:, k : k + width] if sums is None else sums + back[:, k : k + width]
        total = high_sum[:, :width] + high_sum[:, width:] + low_sum[:, :width]
        own_high, own_low = feat[:, :width].astype(F32), feat[:, 2 * width : 3 * width].astype(F32)
        total = total - jnp.sum(sums, axis=1, keepdims=True) * (own_high + own_low) - low_sum[:, width:] * own_high
        if acc_ref is not None:
            total = acc_ref[pl.ds(acc_start + i * rows, rows), :] + total
        if more_ref is not None:
            total = more_ref[pl.ds(i * rows, rows), :] + total
        out_ref[pl.ds(i * rows, rows), :] = total

    for i in range(out_ref.shape[0] // rows):
        chunk(i, i == 0)


def pairs(feat, fac, units, acc=None, start=0, rows=None, acc_start=0, more=None):
    width = feat.shape[1] // 4
    rows = feat.shape[0] if rows is None else rows
    kinds = [isinstance(x, tuple) for x in units]
    arrays = [y for x in units for y in (x if isinstance(x, tuple) else (x,))]
    count = sum((x[0] if isinstance(x, tuple) else x).shape[0] for x in units)
    has_acc = acc is not None
    return call(
        functools.partial(pair_kernel, kinds, has_acc, more is not None, start, start - acc_start),
        "pair_terms",
        jax.ShapeDtypeStruct((rows, width), F32),
        feat,
        fac,
        *arrays,
        *([acc] if has_acc else []),
        *([more] if more is not None else []),
        scratch=[pltpu.VMEM((count, 4 * width), BF16), pltpu.VMEM((count, 2 * width), BF16)],
        pairs=rows * count,
        aliases={2 + len(arrays): 0} if has_acc and rows == acc.shape[0] else None,
    )


def ring_order(homes):
    if homes % 2:
        return list(range(homes))
    return list(range(0, homes, 2)) + list(range(homes - 1, 0, -2))


def body(features, factors):
    replicas = lax.axis_size("rep")
    blocks = lax.axis_size("blk")
    count, width = features.shape
    share = count // replicas
    rep = lax.axis_index("rep")
    rep_ref = rep.astype(jnp.int32).reshape(1)
    homes = blocks // 2
    order = ring_order(homes)
    after = lax.optimization_barrier

    def ring(x):
        moves = []
        for p in range(homes):
            moves += [(order[p] * 2 + c, order[(p + 1 - 2 * c) % homes] * 2 + c) for c in range(2)]
        return lax.ppermute(x, "blk", moves)

    def other_core(x):
        return lax.ppermute(x, "blk", [(b, b ^ 1) for b in range(blocks)])

    slices = after([lax.dynamic_slice_in_dim(x, rep * share, share) for x in (features, factors)])
    own = jnp.concatenate(scale(*slices), axis=1)
    first = ring(own)
    own, features, factors = after((own, features, factors))
    part = share // 2 if replicas <= 2 and share % 32 == 0 else count
    made = own_rows(rep_ref, replicas, features, factors, part)
    filled, parts = made[:2], made[2:]
    own_block = list(zip(parts[::2], parts[1::2], strict=True))
    parts = [other_core(x) for x in parts]
    if part < share:
        beside = [jnp.concatenate(parts[k - 2 * (share // part) :: 2]) for k in (0, 1)]
    else:
        beside = [x[part - share :] for x in parts[-2:]]
    second = ring(jnp.concatenate(beside, axis=1))
    feat, fac = other_rows(share, parts, filled)
    mine_at = 2 * share * (replicas - 1)

    full = (homes - 1) // 2
    total = 2 * full + (homes + 1) % 2
    cut = share // 2 if total > 2 and share % (2 * width) == 0 else 0
    flying, last = [first, second], []
    acc = None
    early = len(own_block) // 2
    mine = pairs(feat, fac, own_block[:early], None, mine_at, 2 * share) if early else None
    for step in range(total - 1):
        here, feat, fac, acc, mine = after((flying[step % 2], feat, fac, acc, mine))
        if step + 2 < total:
            if cut and step + 3 == total:
                last = [ring(here[:cut]), ring(here[cut:])]
            else:
                flying[step % 2] = ring(here)
        if step + 2 < total:
            acc = pairs(feat, fac, [here], acc)
        if step == 0:
            acc, mine = after((acc, mine))
            mine = pairs(feat, fac, own_block[early:], mine, mine_at, 2 * share, mine_at)
    if total < 2:
        mine = pairs(feat, fac, own_block[early:], mine, mine_at, 2 * share, mine_at)
    last = last or [flying[(total - 1) % 2]]
    late = [here, *last] if total > 1 else last

    theirs = acc
    for x in late[:-1] if mine_at else []:
        x, theirs = after((x, theirs))
        theirs = pairs(feat, fac, [x], theirs, 0, mine_at)
    end, theirs, acc = after((late[-1], theirs, acc))
    late = [*late[:-1], end]
    arrived = []
    for k in range(replicas - 1):
        at = k * 2 * share
        received = other_core(pairs(feat, fac, [end], theirs, at, share))
        part = pairs(feat, fac, [end], theirs, at + share, share) + received
        arrived.append(lax.ppermute(part, "rep", [(r, (r + k + 1) % replicas) for r in range(replicas)]))
        acc, part = after((acc, part))
    part = pairs(feat, fac, late, acc, mine_at, 2 * share, 0, mine)
    half = share // 2
    part = part[share:] + jnp.concatenate([other_core(part[:half]), other_core(part[half:share])])
    for x in arrived:
        part = part + x
    return part * (1.0 / (width * math.sqrt(math.log2(math.e) / width)))


def solution(mesh):
    placed = (P("blk", None), P("blk", None))
    return jax.shard_map(
        body, mesh=mesh, in_specs=placed, out_specs=P(("blk", "rep"), None), check_vma=False
    )
```

```python
import functools
import math

import jax
import jax.numpy as jnp
from jax import lax
from jax.experimental import pallas as pl
from jax.experimental.pallas import tpu as pltpu
from jax.sharding import PartitionSpec as P

F32, BF16 = jnp.float32, jnp.bfloat16
NT = (((1,), (1,)), ((), ()))
VMEM_LIMIT = 16 << 20
IN_VMEM = pl.BlockSpec(memory_space=pltpu.VMEM)


def split(x):
    high = x.astype(BF16)
    low = (x - high.astype(F32)).astype(BF16)
    return high, low


def call(kernel, name, out, *args, scratch=(), pairs=0, aliases=None):
    width = 128
    return pl.pallas_call(
        kernel,
        in_specs=[IN_VMEM] * len(args),
        out_specs=jax.tree.map(lambda _: IN_VMEM, out),
        out_shape=out,
        scratch_shapes=scratch,
        input_output_aliases=aliases or {},
        compiler_params=pltpu.CompilerParams(vmem_limit_bytes=VMEM_LIMIT),
        cost_estimate=pl.CostEstimate(flops=2 * pairs * 12 * width, bytes_accessed=4 << 20, transcendentals=pairs),
        name=name,
    )(*args)


def scale(feat, fac):
    width = feat.shape[1]
    feat = feat * math.sqrt(math.log2(math.e) / width)
    norm = jnp.sum(feat * feat, axis=1, keepdims=True)
    return feat, fac * jnp.exp2(-0.5 * norm)


def store_split(out, at, x):
    parts = split(x)
    for k in range(4):
        out[at, k * x.shape[1] : (k + 1) * x.shape[1]] = parts[k // 2]


def own_rows_kernel(replicas, rep_ref, feat_ref, fac_ref, feat_out, fac_out, *parts):
    count = feat_ref.shape[0]
    share = count // replicas
    for k in range(replicas):
        here = pl.ds(pl.multiple_of(lax.rem(rep_ref[0] + 1 + k, replicas) * share, share), share)
        values = scale(feat_ref[here, :], fac_ref[here, :])
        for x, out, held in zip(values, (feat_out, fac_out), (parts[::2], parts[1::2]), strict=True):
            store_split(out, pl.ds((2 * k + 1) * share, share), x)
            rows = min(share, held[0].shape[0])
            for first in range(0, share, rows):
                part, at = divmod(k * share + first, held[0].shape[0])
                held[part][at : at + rows, :] = x[first : first + rows, :]


def own_rows(rep, replicas, feat, fac, part):
    count, width = feat.shape
    split_out = jax.ShapeDtypeStruct((2 * count, 4 * width), BF16)
    outs = [split_out] * 2 + [jax.ShapeDtypeStruct((part, width), F32)] * (2 * (count // part))
    return pl.pallas_call(
        functools.partial(own_rows_kernel, replicas),
        in_specs=[pl.BlockSpec(memory_space=pltpu.SMEM)] + [IN_VMEM] * 2,
        out_specs=[IN_VMEM] * len(outs),
        out_shape=outs,
        compiler_params=pltpu.CompilerParams(vmem_limit_bytes=VMEM_LIMIT),
        name="own_rows",
    )(rep, feat, fac)


def other_rows_kernel(share, n_parts, *refs):
    outs = refs[-2:]
    held = refs[0].shape[0]
    rows = min(share, held)
    for part in range(n_parts):
        for first in range(0, held, rows):
            k, at = divmod(part * held + first, share)
            for out, x in zip(outs, refs[2 * part : 2 * part + 2], strict=True):
                store_split(out, pl.ds(2 * k * share + at, rows), x[first : first + rows, :])


def other_rows(share, parts, filled):
    n_parts = len(parts) // 2
    return pl.pallas_call(
        functools.partial(other_rows_kernel, share, n_parts),
        in_specs=[IN_VMEM] * (len(parts) + 2),
        out_specs=[IN_VMEM] * 2,
        out_shape=[jax.ShapeDtypeStruct(x.shape, x.dtype) for x in filled],
        input_output_aliases={len(parts): 0, len(parts) + 1: 1},
        compiler_params=pltpu.CompilerParams(vmem_limit_bytes=VMEM_LIMIT),
        name="other_rows",
    )(*parts, *filled)


def pair_kernel(kinds, has_acc, has_more, start, acc_start, *refs):
    feat_ref, fac_ref, *refs = refs
    value, coup_rhs = refs[-2:]
    out_ref = refs[-3]
    more_ref = refs[-4] if has_more else None
    acc_ref = refs[-4 - has_more] if has_acc else None
    width = out_ref.shape[1]
    tiles = []
    for pair in kinds:
        feat, fac, refs = (refs[0], refs[1], refs[2:]) if pair else (refs[0], refs[0], refs[1:])
        tile = math.gcd(256, feat.shape[0])
        tiles += [(feat, fac, at, tile, pair) for at in range(0, feat.shape[0], tile)]
    rows = math.gcd(1024, out_ref.shape[0])

    def dot_nt(a, b):
        return lax.dot_general(a, b, NT, preferred_element_type=F32)

    def place(k):
        first = sum(t[3] for t in tiles[:k])
        return slice(first, first + tiles[k][3])

    def prepare(k):
        feat, fac, at, tile, pair = tiles[k]
        here, at = place(k), slice(at, at + tile)
        high, low = split(feat[at, :width])
        value[here, :] = jnp.concatenate([high, low, high, jnp.ones_like(high)], axis=1)
        fac = fac[at, :] if pair else fac[at, width:]
        high, low = split(jnp.concatenate([fac[:, width // 2 :], fac[:, : width // 2]], axis=1))
        coup_rhs[here, :] = jnp.concatenate([high, low], axis=1)

    def chunk(i, first):
        own = pl.ds(start + i * rows, rows)
        feat, fac = feat_ref[own, :], fac_ref[own, :]
        high_sum, low_sum, sums = None, None, None
        for k in range(len(tiles)):
            if first:
                prepare(k)
            here = place(k)
            both, other = value[here, : 2 * width], coup_rhs[here, :]
            cross = dot_nt(feat[:, : 2 * width], both) + dot_nt(feat[:, 2 * width :], both)
            coup = dot_nt(fac[:, : 2 * width], other) + dot_nt(fac[:, 2 * width :], other)
            weight = jnp.exp2(cross) * coup
            high = weight.astype(BF16)
            back = high.astype(F32)
            low = (weight - back).astype(BF16)
            a = jnp.dot(high, both, preferred_element_type=F32)
            b = jnp.dot(low, value[here, 2 * width :], preferred_element_type=F32)
            high_sum = a if high_sum is None else high_sum + a
            low_sum = b if low_sum is None else low_sum + b
            for k in range(0, weight.shape[1], width):
                sums = back[:, k : k + width] if sums is None else sums + back[:, k : k + width]
        total = high_sum[:, :width] + high_sum[:, width:] + low_sum[:, :width]
        own_high, own_low = feat[:, :width].astype(F32), feat[:, 2 * width : 3 * width].astype(F32)
        total = total - jnp.sum(sums, axis=1, keepdims=True) * (own_high + own_low) - low_sum[:, width:] * own_high
        if acc_ref is not None:
            total = acc_ref[pl.ds(acc_start + i * rows, rows), :] + total
        if more_ref is not None:
            total = more_ref[pl.ds(i * rows, rows), :] + total
        out_ref[pl.ds(i * rows, rows), :] = total

    for i in range(out_ref.shape[0] // rows):
        chunk(i, i == 0)


def pairs(feat, fac, units, acc=None, start=0, rows=None, acc_start=0, more=None):
    width = feat.shape[1] // 4
    rows = feat.shape[0] if rows is None else rows
    kinds = [isinstance(x, tuple) for x in units]
    arrays = [y for x in units for y in (x if isinstance(x, tuple) else (x,))]
    count = sum((x[0] if isinstance(x, tuple) else x).shape[0] for x in units)
    has_acc = acc is not None
    return call(
        functools.partial(pair_kernel, kinds, has_acc, more is not None, start, start - acc_start),
        "pair_terms",
        jax.ShapeDtypeStruct((rows, width), F32),
        feat,
        fac,
        *arrays,
        *([acc] if has_acc else []),
        *([more] if more is not None else []),
        scratch=[pltpu.VMEM((count, 4 * width), BF16), pltpu.VMEM((count, 2 * width), BF16)],
        pairs=rows * count,
        aliases={2 + len(arrays): 0} if has_acc and rows == acc.shape[0] else None,
    )


def ring_order(homes):
    if homes % 2:
        return list(range(homes))
    return list(range(0, homes, 2)) + list(range(homes - 1, 0, -2))


def body(features, factors):
    replicas = lax.axis_size("rep")
    blocks = lax.axis_size("blk")
    count, width = features.shape
    share = count // replicas
    rep = lax.axis_index("rep")
    rep_ref = rep.astype(jnp.int32).reshape(1)
    homes = blocks // 2
    order = ring_order(homes)
    after = lax.optimization_barrier

    def ring(x):
        moves = []
        for p in range(homes):
            moves += [(order[p] * 2 + c, order[(p + 1 - 2 * c) % homes] * 2 + c) for c in range(2)]
        return lax.ppermute(x, "blk", moves)

    def other_core(x):
        return lax.ppermute(x, "blk", [(b, b ^ 1) for b in range(blocks)])

    def scaled(x):
        return jnp.concatenate(scale(x[:, :width], x[:, width:]), axis=1)

    slices = after([lax.dynamic_slice_in_dim(x, rep * share, share) for x in (features, factors)])
    own = jnp.concatenate(slices, axis=1)
    first = ring(own)
    own, features, factors = after((own, features, factors))
    part = share // 2 if replicas <= 2 and share % 32 == 0 else count
    made = own_rows(rep_ref, replicas, features, factors, part)
    filled, parts = made[:2], made[2:]
    own_block = list(zip(parts[::2], parts[1::2], strict=True))
    parts = [other_core(x) for x in parts]
    if part < share:
        beside = [jnp.concatenate(parts[k - 2 * (share // part) :: 2]) for k in (0, 1)]
    else:
        beside = [x[part - share :] for x in parts[-2:]]
    second = ring(jnp.concatenate(beside, axis=1))
    feat, fac = other_rows(share, parts, filled)
    mine_at = 2 * share * (replicas - 1)

    full = (homes - 1) // 2
    total = 2 * full + (homes + 1) % 2
    cut = share // 2 if total > 2 and share % (2 * width) == 0 else 0
    flying, last = [first, second], []
    acc = None
    early = len(own_block) // 2
    mine = pairs(feat, fac, own_block[:early], None, mine_at, 2 * share) if early else None
    for step in range(total - 1):
        here, feat, fac, acc, mine = after((flying[step % 2], feat, fac, acc, mine))
        if step == 0:
            here = scaled(here)
        if step + 2 < total:
            if cut and step + 3 == total:
                last = [ring(here[:cut]), ring(here[cut:])]
            else:
                flying[step % 2] = ring(here)
        if step + 2 < total:
            acc = pairs(feat, fac, [here], acc)
        if step == 0:
            acc, mine = after((acc, mine))
            mine = pairs(feat, fac, own_block[early:], mine, mine_at, 2 * share, mine_at)
    if total < 2:
        mine = pairs(feat, fac, own_block[early:], mine, mine_at, 2 * share, mine_at)
    last = last or [flying[(total - 1) % 2] if total > 1 else scaled(first)]
    late = [here, *last] if total > 1 else last

    theirs = acc
    for x in late[:-1] if mine_at else []:
        x, theirs = after((x, theirs))
        theirs = pairs(feat, fac, [x], theirs, 0, mine_at)
    end, theirs, acc = after((late[-1], theirs, acc))
    late = [*late[:-1], end]
    arrived = []
    for k in range(replicas - 1):
        at = k * 2 * share
        received = other_core(pairs(feat, fac, [end], theirs, at, share))
        part = pairs(feat, fac, [end], theirs, at + share, share) + received
        arrived.append(lax.ppermute(part, "rep", [(r, (r + k + 1) % replicas) for r in range(replicas)]))
        acc, part = after((acc, part))
    part = pairs(feat, fac, late, acc, mine_at, 2 * share, 0, mine)
    half = share // 2
    part = part[share:] + jnp.concatenate([other_core(part[:half]), other_core(part[half:share])])
    for x in arrived:
        part = part + x
    return part * (1.0 / (width * math.sqrt(math.log2(math.e) / width)))


def solution(mesh):
    placed = (P("blk", None), P("blk", None))
    return jax.shard_map(
        body, mesh=mesh, in_specs=placed, out_specs=P(("blk", "rep"), None), check_vma=False
    )
```

```python
import functools
import math

import jax
import jax.numpy as jnp
from jax import lax
from jax.experimental import pallas as pl
from jax.experimental.pallas import tpu as pltpu
from jax.sharding import PartitionSpec as P

F32, BF16 = jnp.float32, jnp.bfloat16
NT = (((1,), (1,)), ((), ()))
VMEM_LIMIT = 16 << 20
IN_VMEM = pl.BlockSpec(memory_space=pltpu.VMEM)


def split(x):
    high = x.astype(BF16)
    low = (x - high.astype(F32)).astype(BF16)
    return high, low


def call(kernel, name, out, *args, scratch=(), pairs=0, aliases=None):
    width = 128
    return pl.pallas_call(
        kernel,
        in_specs=[IN_VMEM] * len(args),
        out_specs=jax.tree.map(lambda _: IN_VMEM, out),
        out_shape=out,
        scratch_shapes=scratch,
        input_output_aliases=aliases or {},
        compiler_params=pltpu.CompilerParams(vmem_limit_bytes=VMEM_LIMIT),
        cost_estimate=pl.CostEstimate(flops=2 * pairs * 12 * width, bytes_accessed=4 << 20, transcendentals=pairs),
        name=name,
    )(*args)


def scale(feat, fac):
    width = feat.shape[1]
    feat = feat * math.sqrt(math.log2(math.e) / width)
    norm = jnp.sum(feat * feat, axis=1, keepdims=True)
    return feat, fac * jnp.exp2(-0.5 * norm)


def store_split(out, at, x):
    parts = split(x)
    for k in range(4):
        out[at, k * x.shape[1] : (k + 1) * x.shape[1]] = parts[k // 2]


def own_rows_kernel(replicas, rep_ref, feat_ref, fac_ref, feat_out, fac_out, *parts):
    count = feat_ref.shape[0]
    share = count // replicas
    for k in range(replicas):
        here = pl.ds(pl.multiple_of(lax.rem(rep_ref[0] + 1 + k, replicas) * share, share), share)
        values = scale(feat_ref[here, :], fac_ref[here, :])
        for x, out, held in zip(values, (feat_out, fac_out), (parts[::2], parts[1::2]), strict=True):
            store_split(out, pl.ds((2 * k + 1) * share, share), x)
            rows = min(share, held[0].shape[0])
            for first in range(0, share, rows):
                part, at = divmod(k * share + first, held[0].shape[0])
                held[part][at : at + rows, :] = x[first : first + rows, :]


def own_rows(rep, replicas, feat, fac, part):
    count, width = feat.shape
    split_out = jax.ShapeDtypeStruct((2 * count, 4 * width), BF16)
    outs = [split_out] * 2 + [jax.ShapeDtypeStruct((part, width), F32)] * (2 * (count // part))
    return pl.pallas_call(
        functools.partial(own_rows_kernel, replicas),
        in_specs=[pl.BlockSpec(memory_space=pltpu.SMEM)] + [IN_VMEM] * 2,
        out_specs=[IN_VMEM] * len(outs),
        out_shape=outs,
        compiler_params=pltpu.CompilerParams(vmem_limit_bytes=VMEM_LIMIT),
        name="own_rows",
    )(rep, feat, fac)


def other_rows_kernel(share, n_parts, *refs):
    outs = refs[-2:]
    held = refs[0].shape[0]
    rows = min(share, held)
    for part in range(n_parts):
        for first in range(0, held, rows):
            k, at = divmod(part * held + first, share)
            for out, x in zip(outs, refs[2 * part : 2 * part + 2], strict=True):
                store_split(out, pl.ds(2 * k * share + at, rows), x[first : first + rows, :])


def other_rows(share, parts, filled):
    n_parts = len(parts) // 2
    return pl.pallas_call(
        functools.partial(other_rows_kernel, share, n_parts),
        in_specs=[IN_VMEM] * (len(parts) + 2),
        out_specs=[IN_VMEM] * 2,
        out_shape=[jax.ShapeDtypeStruct(x.shape, x.dtype) for x in filled],
        input_output_aliases={len(parts): 0, len(parts) + 1: 1},
        compiler_params=pltpu.CompilerParams(vmem_limit_bytes=VMEM_LIMIT),
        name="other_rows",
    )(*parts, *filled)


def pair_kernel(kinds, has_acc, has_more, start, acc_start, *refs):
    feat_ref, fac_ref, *refs = refs
    value, coup_rhs = refs[-2:]
    out_ref = refs[-3]
    more_ref = refs[-4] if has_more else None
    acc_ref = refs[-4 - has_more] if has_acc else None
    width = out_ref.shape[1]
    tiles = []
    for pair in kinds:
        feat, fac, refs = (refs[0], refs[1], refs[2:]) if pair else (refs[0], refs[0], refs[1:])
        tile = math.gcd(256, feat.shape[0])
        tiles += [(feat, fac, at, tile, pair) for at in range(0, feat.shape[0], tile)]
    rows = math.gcd(1024, out_ref.shape[0])

    def dot_nt(a, b):
        return lax.dot_general(a, b, NT, preferred_element_type=F32)

    def place(k):
        first = sum(t[3] for t in tiles[:k])
        return slice(first, first + tiles[k][3])

    def prepare(k):
        feat, fac, at, tile, pair = tiles[k]
        here, at = place(k), slice(at, at + tile)
        high, low = split(feat[at, :width])
        value[here, :] = jnp.concatenate([high, low, high, jnp.ones_like(high)], axis=1)
        fac = fac[at, :] if pair else fac[at, width:]
        high, low = split(jnp.concatenate([fac[:, width // 2 :], fac[:, : width // 2]], axis=1))
        coup_rhs[here, :] = jnp.concatenate([high, low], axis=1)

    def chunk(i, first):
        own = pl.ds(start + i * rows, rows)
        feat, fac = feat_ref[own, :], fac_ref[own, :]
        high_sum, low_sum, sums = None, None, None
        for k in range(len(tiles)):
            if first:
                prepare(k)
            here = place(k)
            both, other = value[here, : 2 * width], coup_rhs[here, :]
            cross = dot_nt(feat[:, : 2 * width], both) + dot_nt(feat[:, 2 * width :], both)
            coup = dot_nt(fac[:, : 2 * width], other) + dot_nt(fac[:, 2 * width :], other)
            weight = jnp.exp2(cross) * coup
            high = weight.astype(BF16)
            back = high.astype(F32)
            low = (weight - back).astype(BF16)
            a = jnp.dot(high, both, preferred_element_type=F32)
            b = jnp.dot(low, value[here, 2 * width :], preferred_element_type=F32)
            high_sum = a if high_sum is None else high_sum + a
            low_sum = b if low_sum is None else low_sum + b
            for k in range(0, weight.shape[1], width):
                sums = back[:, k : k + width] if sums is None else sums + back[:, k : k + width]
        total = high_sum[:, :width] + high_sum[:, width:] + low_sum[:, :width]
        own_high, own_low = feat[:, :width].astype(F32), feat[:, 2 * width : 3 * width].astype(F32)
        total = total - jnp.sum(sums, axis=1, keepdims=True) * (own_high + own_low) - low_sum[:, width:] * own_high
        if acc_ref is not None:
            total = acc_ref[pl.ds(acc_start + i * rows, rows), :] + total
        if more_ref is not None:
            total = more_ref[pl.ds(i * rows, rows), :] + total
        out_ref[pl.ds(i * rows, rows), :] = total

    for i in range(out_ref.shape[0] // rows):
        chunk(i, i == 0)


def pairs(feat, fac, units, acc=None, start=0, rows=None, acc_start=0, more=None):
    width = feat.shape[1] // 4
    rows = feat.shape[0] if rows is None else rows
    kinds = [isinstance(x, tuple) for x in units]
    arrays = [y for x in units for y in (x if isinstance(x, tuple) else (x,))]
    count = sum((x[0] if isinstance(x, tuple) else x).shape[0] for x in units)
    has_acc = acc is not None
    return call(
        functools.partial(pair_kernel, kinds, has_acc, more is not None, start, start - acc_start),
        "pair_terms",
        jax.ShapeDtypeStruct((rows, width), F32),
        feat,
        fac,
        *arrays,
        *([acc] if has_acc else []),
        *([more] if more is not None else []),
        scratch=[pltpu.VMEM((count, 4 * width), BF16), pltpu.VMEM((count, 2 * width), BF16)],
        pairs=rows * count,
        aliases={2 + len(arrays): 0} if has_acc and rows == acc.shape[0] else None,
    )


def ring_order(homes):
    if homes % 2:
        return list(range(homes))
    return list(range(0, homes, 2)) + list(range(homes - 1, 0, -2))


def body(features, factors):
    replicas = lax.axis_size("rep")
    blocks = lax.axis_size("blk")
    count, width = features.shape
    share = count // replicas
    rep = lax.axis_index("rep")
    rep_ref = rep.astype(jnp.int32).reshape(1)
    homes = blocks // 2
    order = ring_order(homes)
    after = lax.optimization_barrier

    def ring(x):
        moves = []
        for p in range(homes):
            for c in range(2):
                onward = (p + c) % 2 == 0 if homes % 2 == 0 else c == 0
                core = 1 - c if homes % 2 == 0 else c
                moves.append((order[p] * 2 + c, order[(p + (1 if onward else -1)) % homes] * 2 + core))
        return lax.ppermute(x, "blk", moves)

    def other_core(x):
        return lax.ppermute(x, "blk", [(b, b ^ 1) for b in range(blocks)])

    def scaled(x):
        return jnp.concatenate(scale(x[:, :width], x[:, width:]), axis=1)

    slices = after([lax.dynamic_slice_in_dim(x, rep * share, share) for x in (features, factors)])
    own = jnp.concatenate(slices, axis=1)
    first = ring(own)
    own, features, factors = after((own, features, factors))
    part = share // 2 if replicas <= 2 and share % 32 == 0 else count
    made = own_rows(rep_ref, replicas, features, factors, part)
    filled, parts = made[:2], made[2:]
    own_block = list(zip(parts[::2], parts[1::2], strict=True))
    parts = [other_core(x) for x in parts]
    if part < share:
        beside = [jnp.concatenate(parts[k - 2 * (share // part) :: 2]) for k in (0, 1)]
    else:
        beside = [x[part - share :] for x in parts[-2:]]
    second = ring(jnp.concatenate(beside, axis=1))
    feat, fac = other_rows(share, parts, filled)
    mine_at = 2 * share * (replicas - 1)

    full = (homes - 1) // 2
    total = 2 * full + (homes + 1) % 2
    cut = share // 2 if total > 2 and share % (2 * width) == 0 else 0
    flying, last = [first, second], []
    acc = None
    early = len(own_block) // 2
    mine = pairs(feat, fac, own_block[:early], None, mine_at, 2 * share) if early else None
    for step in range(total - 1):
        here, feat, fac, acc, mine = after((flying[step % 2], feat, fac, acc, mine))
        if step == 0:
            here = scaled(here)
        if step + 2 < total:
            if cut and step + 3 == total:
                last = [ring(here[:cut]), ring(here[cut:])]
            else:
                flying[step % 2] = ring(here)
        if step + 2 < total:
            acc = pairs(feat, fac, [here], acc)
        if step == 0:
            acc, mine = after((acc, mine))
            mine = pairs(feat, fac, own_block[early:], mine, mine_at, 2 * share, mine_at)
    if total < 2:
        mine = pairs(feat, fac, own_block[early:], mine, mine_at, 2 * share, mine_at)
    last = last or [flying[(total - 1) % 2] if total > 1 else scaled(first)]
    late = [here, *last] if total > 1 else last

    theirs = acc
    for x in late[:-1] if mine_at else []:
        x, theirs = after((x, theirs))
        theirs = pairs(feat, fac, [x], theirs, 0, mine_at)
    end, theirs, acc = after((late[-1], theirs, acc))
    late = [*late[:-1], end]
    arrived = []
    for k in range(replicas - 1):
        at = k * 2 * share
        received = other_core(pairs(feat, fac, [end], theirs, at, share))
        part = pairs(feat, fac, [end], theirs, at + share, share) + received
        arrived.append(lax.ppermute(part, "rep", [(r, (r + k + 1) % replicas) for r in range(replicas)]))
        acc, part = after((acc, part))
    part = pairs(feat, fac, late, acc, mine_at, 2 * share, 0, mine)
    half = share // 2
    part = part[share:] + jnp.concatenate([other_core(part[:half]), other_core(part[half:share])])
    for x in arrived:
        part = part + x
    return part * (1.0 / (width * math.sqrt(math.log2(math.e) / width)))


def solution(mesh):
    placed = (P("blk", None), P("blk", None))
    return jax.shard_map(
        body, mesh=mesh, in_specs=placed, out_specs=P(("blk", "rep"), None), check_vma=False
    )
```

```python
import functools
import math

import jax
import jax.numpy as jnp
from jax import lax
from jax.experimental import pallas as pl
from jax.experimental.pallas import tpu as pltpu
from jax.sharding import PartitionSpec as P

F32, BF16 = jnp.float32, jnp.bfloat16
NT = (((1,), (1,)), ((), ()))
VMEM_LIMIT = 16 << 20
IN_VMEM = pl.BlockSpec(memory_space=pltpu.VMEM)


def split(x):
    high = x.astype(BF16)
    low = (x - high.astype(F32)).astype(BF16)
    return high, low


def call(kernel, name, out, *args, scratch=(), pairs=0, aliases=None):
    width = 128
    return pl.pallas_call(
        kernel,
        in_specs=[IN_VMEM] * len(args),
        out_specs=jax.tree.map(lambda _: IN_VMEM, out),
        out_shape=out,
        scratch_shapes=scratch,
        input_output_aliases=aliases or {},
        compiler_params=pltpu.CompilerParams(vmem_limit_bytes=VMEM_LIMIT),
        cost_estimate=pl.CostEstimate(flops=2 * pairs * 12 * width, bytes_accessed=4 << 20, transcendentals=pairs),
        name=name,
    )(*args)


def scale(feat, fac):
    width = feat.shape[1]
    feat = feat * math.sqrt(math.log2(math.e) / width)
    norm = jnp.sum(feat * feat, axis=1, keepdims=True)
    return feat, fac * jnp.exp2(-0.5 * norm)


def store_split(out, at, x):
    parts = split(x)
    for k in range(4):
        out[at, k * x.shape[1] : (k + 1) * x.shape[1]] = parts[k // 2]


def own_rows_kernel(replicas, rep_ref, feat_ref, fac_ref, feat_out, fac_out, *parts):
    count = feat_ref.shape[0]
    share = count // replicas
    for k in range(replicas):
        here = pl.ds(pl.multiple_of(lax.rem(rep_ref[0] + 1 + k, replicas) * share, share), share)
        values = scale(feat_ref[here, :], fac_ref[here, :])
        for x, out, held in zip(values, (feat_out, fac_out), (parts[::2], parts[1::2]), strict=True):
            store_split(out, pl.ds((2 * k + 1) * share, share), x)
            rows = min(share, held[0].shape[0])
            for first in range(0, share, rows):
                part, at = divmod(k * share + first, held[0].shape[0])
                held[part][at : at + rows, :] = x[first : first + rows, :]


def own_rows(rep, replicas, feat, fac, part):
    count, width = feat.shape
    split_out = jax.ShapeDtypeStruct((2 * count, 4 * width), BF16)
    outs = [split_out] * 2 + [jax.ShapeDtypeStruct((part, width), F32)] * (2 * (count // part))
    return pl.pallas_call(
        functools.partial(own_rows_kernel, replicas),
        in_specs=[pl.BlockSpec(memory_space=pltpu.SMEM)] + [IN_VMEM] * 2,
        out_specs=[IN_VMEM] * len(outs),
        out_shape=outs,
        compiler_params=pltpu.CompilerParams(vmem_limit_bytes=VMEM_LIMIT),
        name="own_rows",
    )(rep, feat, fac)


def other_rows_kernel(share, n_parts, *refs):
    outs = refs[-2:]
    held = refs[0].shape[0]
    rows = min(share, held)
    for part in range(n_parts):
        for first in range(0, held, rows):
            k, at = divmod(part * held + first, share)
            for out, x in zip(outs, refs[2 * part : 2 * part + 2], strict=True):
                store_split(out, pl.ds(2 * k * share + at, rows), x[first : first + rows, :])


def other_rows(share, parts, filled):
    n_parts = len(parts) // 2
    return pl.pallas_call(
        functools.partial(other_rows_kernel, share, n_parts),
        in_specs=[IN_VMEM] * (len(parts) + 2),
        out_specs=[IN_VMEM] * 2,
        out_shape=[jax.ShapeDtypeStruct(x.shape, x.dtype) for x in filled],
        input_output_aliases={len(parts): 0, len(parts) + 1: 1},
        compiler_params=pltpu.CompilerParams(vmem_limit_bytes=VMEM_LIMIT),
        name="other_rows",
    )(*parts, *filled)


def pair_kernel(kinds, has_acc, has_more, start, acc_start, *refs):
    feat_ref, fac_ref, *refs = refs
    value, coup_rhs = refs[-2:]
    out_ref = refs[-3]
    more_ref = refs[-4] if has_more else None
    acc_ref = refs[-4 - has_more] if has_acc else None
    width = out_ref.shape[1]
    tiles = []
    for pair in kinds:
        feat, fac, refs = (refs[0], refs[1], refs[2:]) if pair else (refs[0], refs[0], refs[1:])
        tile = math.gcd(256, feat.shape[0])
        tiles += [(feat, fac, at, tile, pair) for at in range(0, feat.shape[0], tile)]
    rows = math.gcd(1024, out_ref.shape[0])

    def dot_nt(a, b):
        return lax.dot_general(a, b, NT, preferred_element_type=F32)

    def place(k):
        first = sum(t[3] for t in tiles[:k])
        return slice(first, first + tiles[k][3])

    def prepare(k):
        feat, fac, at, tile, pair = tiles[k]
        here, at = place(k), slice(at, at + tile)
        high, low = split(feat[at, :width])
        value[here, :] = jnp.concatenate([high, low, high, jnp.ones_like(high)], axis=1)
        fac = fac[at, :] if pair else fac[at, width:]
        high, low = split(jnp.concatenate([fac[:, width // 2 :], fac[:, : width // 2]], axis=1))
        coup_rhs[here, :] = jnp.concatenate([high, low], axis=1)

    def chunk(i, first):
        own = pl.ds(start + i * rows, rows)
        feat, fac = feat_ref[own, :], fac_ref[own, :]
        high_sum, low_sum, sums = None, None, None
        for k in range(len(tiles)):
            if first:
                prepare(k)
            here = place(k)
            both, other = value[here, : 2 * width], coup_rhs[here, :]
            cross = dot_nt(feat[:, : 2 * width], both) + dot_nt(feat[:, 2 * width :], both)
            coup = dot_nt(fac[:, : 2 * width], other) + dot_nt(fac[:, 2 * width :], other)
            weight = jnp.exp2(cross) * coup
            high = weight.astype(BF16)
            back = high.astype(F32)
            low = (weight - back).astype(BF16)
            a = jnp.dot(high, both, preferred_element_type=F32)
            b = jnp.dot(low, value[here, 2 * width :], preferred_element_type=F32)
            high_sum = a if high_sum is None else high_sum + a
            low_sum = b if low_sum is None else low_sum + b
            for k in range(0, weight.shape[1], width):
                sums = back[:, k : k + width] if sums is None else sums + back[:, k : k + width]
        total = high_sum[:, :width] + high_sum[:, width:] + low_sum[:, :width]
        own_high, own_low = feat[:, :width].astype(F32), feat[:, 2 * width : 3 * width].astype(F32)
        total = total - jnp.sum(sums, axis=1, keepdims=True) * (own_high + own_low) - low_sum[:, width:] * own_high
        if acc_ref is not None:
            total = acc_ref[pl.ds(acc_start + i * rows, rows), :] + total
        if more_ref is not None:
            total = more_ref[pl.ds(i * rows, rows), :] + total
        out_ref[pl.ds(i * rows, rows), :] = total

    for i in range(out_ref.shape[0] // rows):
        chunk(i, i == 0)


def pairs(feat, fac, units, acc=None, start=0, rows=None, acc_start=0, more=None):
    width = feat.shape[1] // 4
    rows = feat.shape[0] if rows is None else rows
    kinds = [isinstance(x, tuple) for x in units]
    arrays = [y for x in units for y in (x if isinstance(x, tuple) else (x,))]
    count = sum((x[0] if isinstance(x, tuple) else x).shape[0] for x in units)
    has_acc = acc is not None
    return call(
        functools.partial(pair_kernel, kinds, has_acc, more is not None, start, start - acc_start),
        "pair_terms",
        jax.ShapeDtypeStruct((rows, width), F32),
        feat,
        fac,
        *arrays,
        *([acc] if has_acc else []),
        *([more] if more is not None else []),
        scratch=[pltpu.VMEM((count, 4 * width), BF16), pltpu.VMEM((count, 2 * width), BF16)],
        pairs=rows * count,
        aliases={2 + len(arrays): 0} if has_acc and rows == acc.shape[0] else None,
    )


def ring_order(homes):
    if homes % 2:
        return list(range(homes))
    return list(range(0, homes, 2)) + list(range(homes - 1, 0, -2))


def body(features, factors):
    replicas = lax.axis_size("rep")
    blocks = lax.axis_size("blk")
    count, width = features.shape
    share = count // replicas
    rep = lax.axis_index("rep")
    rep_ref = rep.astype(jnp.int32).reshape(1)
    homes = blocks // 2
    order = ring_order(homes)
    after = lax.optimization_barrier

    def ring(x):
        moves = []
        for p in range(homes):
            for c in range(2):
                onward = (p + c) % 2 == 0 if homes % 2 == 0 else c == 0
                core = 1 - c if homes % 2 == 0 else c
                moves.append((order[p] * 2 + c, order[(p + (1 if onward else -1)) % homes] * 2 + core))
        return lax.ppermute(x, "blk", moves)

    def other_core(x):
        return lax.ppermute(x, "blk", [(b, b ^ 1) for b in range(blocks)])

    def scaled(x):
        return jnp.concatenate(scale(x[:, :width], x[:, width:]), axis=1)

    slices = after([lax.dynamic_slice_in_dim(x, rep * share, share) for x in (features, factors)])
    own = jnp.concatenate(slices, axis=1)
    first = ring(own)
    own, features, factors = after((own, features, factors))
    part = share // 2 if replicas <= 2 and share % 32 == 0 else count
    made = own_rows(rep_ref, replicas, features, factors, part)
    filled, parts = made[:2], made[2:]
    own_block = list(zip(parts[::2], parts[1::2], strict=True))
    parts = [other_core(x) for x in parts]
    if part < share:
        beside = [jnp.concatenate(parts[k - 2 * (share // part) :: 2]) for k in (0, 1)]
    else:
        beside = [x[part - share :] for x in parts[-2:]]
    second = ring(jnp.concatenate(beside, axis=1))
    feat, fac = other_rows(share, parts, filled)
    mine_at = 2 * share * (replicas - 1)

    full = (homes - 1) // 2
    total = 2 * full + (homes + 1) % 2
    cut = share // 2 if total > 2 and share % (2 * width) == 0 else 0
    flying, last = [first, second], []
    acc = None
    early = len(own_block) // 2
    mine = pairs(feat, fac, own_block[:early], None, mine_at, 2 * share) if early else None
    for step in range(total - 1):
        here, feat, fac, acc, mine = after((flying[step % 2], feat, fac, acc, mine))
        if step == 0:
            here = scaled(here)
        if step + 2 < total:
            if cut and step + 3 == total:
                last = [ring(here[:cut]), ring(here[cut:])]
            else:
                flying[step % 2] = ring(here)
        if step + 2 < total:
            acc = pairs(feat, fac, [here], acc)
        if step == 0:
            acc, mine = after((acc, mine))
            mine = pairs(feat, fac, own_block[early:], mine, mine_at, 2 * share, mine_at)
    if total < 2:
        mine = pairs(feat, fac, own_block[early:], mine, mine_at, 2 * share, mine_at)
    last = last or [flying[(total - 1) % 2] if total > 1 else scaled(first)]
    late = [here, *last] if total > 1 else last

    def across(by):
        return [
            (b * replicas + r, (b ^ 1) * replicas + (r + by) % replicas) for b in range(blocks) for r in range(replicas)
        ]

    theirs = acc
    for x in late[:-1] if mine_at else []:
        x, theirs = after((x, theirs))
        theirs = pairs(feat, fac, [x], theirs, 0, mine_at)
    end, theirs, acc = after((late[-1], theirs, acc))
    late = [*late[:-1], end]
    arrived = []
    for k in range(replicas - 1):
        at = k * 2 * share
        received = other_core(pairs(feat, fac, [end], theirs, at + share, share))
        part = pairs(feat, fac, [end], theirs, at, share) + received
        arrived.append(lax.ppermute(part, ("blk", "rep"), across(k + 1)))
        acc, part = after((acc, part))
    part = pairs(feat, fac, late, acc, mine_at, 2 * share, 0, mine)
    half = share // 2
    part = part[share:] + jnp.concatenate([other_core(part[:half]), other_core(part[half:share])])
    for x in arrived:
        part = part + x
    return part * (1.0 / (width * math.sqrt(math.log2(math.e) / width)))


def solution(mesh):
    placed = (P("blk", None), P("blk", None))
    return jax.shard_map(
        body, mesh=mesh, in_specs=placed, out_specs=P(("blk", "rep"), None), check_vma=False
    )
```

```python
import functools
import math

import jax
import jax.numpy as jnp
from jax import lax
from jax.experimental import pallas as pl
from jax.experimental.pallas import tpu as pltpu
from jax.sharding import PartitionSpec as P

F32, BF16 = jnp.float32, jnp.bfloat16
NT = (((1,), (1,)), ((), ()))
VMEM_LIMIT = 16 << 20
IN_VMEM = pl.BlockSpec(memory_space=pltpu.VMEM)


def split(x):
    high = x.astype(BF16)
    low = (x - high.astype(F32)).astype(BF16)
    return high, low


def call(kernel, name, out, *args, scratch=(), pairs=0, aliases=None):
    width = 128
    return pl.pallas_call(
        kernel,
        in_specs=[IN_VMEM] * len(args),
        out_specs=jax.tree.map(lambda _: IN_VMEM, out),
        out_shape=out,
        scratch_shapes=scratch,
        input_output_aliases=aliases or {},
        compiler_params=pltpu.CompilerParams(vmem_limit_bytes=VMEM_LIMIT),
        cost_estimate=pl.CostEstimate(flops=2 * pairs * 12 * width, bytes_accessed=4 << 20, transcendentals=pairs),
        name=name,
    )(*args)


def scale(feat, fac):
    width = feat.shape[1]
    feat = feat * math.sqrt(math.log2(math.e) / width)
    norm = jnp.sum(feat * feat, axis=1, keepdims=True)
    return feat, fac * jnp.exp2(-0.5 * norm)


def store_split(out, at, x):
    parts = split(x)
    for k in range(4):
        out[at, k * x.shape[1] : (k + 1) * x.shape[1]] = parts[k // 2]


def own_rows_kernel(replicas, rep_ref, feat_ref, fac_ref, feat_out, fac_out, *parts):
    count = feat_ref.shape[0]
    share = count // replicas
    for k in range(replicas):
        here = pl.ds(pl.multiple_of(lax.rem(rep_ref[0] + 1 + k, replicas) * share, share), share)
        values = scale(feat_ref[here, :], fac_ref[here, :])
        for x, out, held in zip(values, (feat_out, fac_out), (parts[::2], parts[1::2]), strict=True):
            store_split(out, pl.ds((2 * k + 1) * share, share), x)
            rows = min(share, held[0].shape[0])
            for first in range(0, share, rows):
                part, at = divmod(k * share + first, held[0].shape[0])
                held[part][at : at + rows, :] = x[first : first + rows, :]


def own_rows(rep, replicas, feat, fac, part):
    count, width = feat.shape
    split_out = jax.ShapeDtypeStruct((2 * count, 4 * width), BF16)
    outs = [split_out] * 2 + [jax.ShapeDtypeStruct((part, width), F32)] * (2 * (count // part))
    return pl.pallas_call(
        functools.partial(own_rows_kernel, replicas),
        in_specs=[pl.BlockSpec(memory_space=pltpu.SMEM)] + [IN_VMEM] * 2,
        out_specs=[IN_VMEM] * len(outs),
        out_shape=outs,
        compiler_params=pltpu.CompilerParams(vmem_limit_bytes=VMEM_LIMIT),
        name="own_rows",
    )(rep, feat, fac)


def other_rows_kernel(share, n_parts, *refs):
    outs = refs[-2:]
    held = refs[0].shape[0]
    rows = min(share, held)
    for part in range(n_parts):
        for first in range(0, held, rows):
            k, at = divmod(part * held + first, share)
            for out, x in zip(outs, refs[2 * part : 2 * part + 2], strict=True):
                store_split(out, pl.ds(2 * k * share + at, rows), x[first : first + rows, :])


def other_rows(share, parts, filled):
    n_parts = len(parts) // 2
    return pl.pallas_call(
        functools.partial(other_rows_kernel, share, n_parts),
        in_specs=[IN_VMEM] * (len(parts) + 2),
        out_specs=[IN_VMEM] * 2,
        out_shape=[jax.ShapeDtypeStruct(x.shape, x.dtype) for x in filled],
        input_output_aliases={len(parts): 0, len(parts) + 1: 1},
        compiler_params=pltpu.CompilerParams(vmem_limit_bytes=VMEM_LIMIT),
        name="other_rows",
    )(*parts, *filled)


def pair_kernel(kinds, has_acc, has_more, start, acc_start, *refs):
    feat_ref, fac_ref, *refs = refs
    value, coup_rhs = refs[-2:]
    out_ref = refs[-3]
    more_ref = refs[-4] if has_more else None
    acc_ref = refs[-4 - has_more] if has_acc else None
    width = out_ref.shape[1]
    tiles = []
    for pair in kinds:
        feat, fac, refs = (refs[0], refs[1], refs[2:]) if pair else (refs[0], refs[0], refs[1:])
        tile = math.gcd(256, feat.shape[0])
        tiles += [(feat, fac, at, tile, pair) for at in range(0, feat.shape[0], tile)]
    rows = math.gcd(1024, out_ref.shape[0])

    def dot_nt(a, b):
        return lax.dot_general(a, b, NT, preferred_element_type=F32)

    def place(k):
        first = sum(t[3] for t in tiles[:k])
        return slice(first, first + tiles[k][3])

    def prepare(k):
        feat, fac, at, tile, pair = tiles[k]
        here, at = place(k), slice(at, at + tile)
        high, low = split(feat[at, :width])
        value[here, :] = jnp.concatenate([high, low, high, jnp.ones_like(high)], axis=1)
        fac = fac[at, :] if pair else fac[at, width:]
        high, low = split(jnp.concatenate([fac[:, width // 2 :], fac[:, : width // 2]], axis=1))
        coup_rhs[here, :] = jnp.concatenate([high, low], axis=1)

    def chunk(i, first):
        own = pl.ds(start + i * rows, rows)
        feat, fac = feat_ref[own, :], fac_ref[own, :]
        high_sum, low_sum, sums = None, None, None
        for k in range(len(tiles)):
            if first:
                prepare(k)
            here = place(k)
            both, other = value[here, : 2 * width], coup_rhs[here, :]
            cross = dot_nt(feat[:, : 2 * width], both) + dot_nt(feat[:, 2 * width :], both)
            coup = dot_nt(fac[:, : 2 * width], other) + dot_nt(fac[:, 2 * width :], other)
            weight = jnp.exp2(cross) * coup
            high = weight.astype(BF16)
            back = high.astype(F32)
            low = (weight - back).astype(BF16)
            a = jnp.dot(high, both, preferred_element_type=F32)
            b = jnp.dot(low, value[here, 2 * width :], preferred_element_type=F32)
            high_sum = a if high_sum is None else high_sum + a
            low_sum = b if low_sum is None else low_sum + b
            for k in range(0, weight.shape[1], width):
                sums = back[:, k : k + width] if sums is None else sums + back[:, k : k + width]
        total = high_sum[:, :width] + high_sum[:, width:] + low_sum[:, :width]
        own_high, own_low = feat[:, :width].astype(F32), feat[:, 2 * width : 3 * width].astype(F32)
        total = total - jnp.sum(sums, axis=1, keepdims=True) * (own_high + own_low) - low_sum[:, width:] * own_high
        if acc_ref is not None:
            total = acc_ref[pl.ds(acc_start + i * rows, rows), :] + total
        if more_ref is not None:
            total = more_ref[pl.ds(i * rows, rows), :] + total
        out_ref[pl.ds(i * rows, rows), :] = total

    for i in range(out_ref.shape[0] // rows):
        chunk(i, i == 0)


def pairs(feat, fac, units, acc=None, start=0, rows=None, acc_start=0, more=None):
    width = feat.shape[1] // 4
    rows = feat.shape[0] if rows is None else rows
    kinds = [isinstance(x, tuple) for x in units]
    arrays = [y for x in units for y in (x if isinstance(x, tuple) else (x,))]
    count = sum((x[0] if isinstance(x, tuple) else x).shape[0] for x in units)
    has_acc = acc is not None
    return call(
        functools.partial(pair_kernel, kinds, has_acc, more is not None, start, start - acc_start),
        "pair_terms",
        jax.ShapeDtypeStruct((rows, width), F32),
        feat,
        fac,
        *arrays,
        *([acc] if has_acc else []),
        *([more] if more is not None else []),
        scratch=[pltpu.VMEM((count, 4 * width), BF16), pltpu.VMEM((count, 2 * width), BF16)],
        pairs=rows * count,
        aliases={2 + len(arrays): 0} if has_acc and rows == acc.shape[0] else None,
    )


def ring_order(homes):
    if homes % 2:
        return list(range(homes))
    return list(range(0, homes, 2)) + list(range(homes - 1, 0, -2))


def body(features, factors):
    replicas = lax.axis_size("rep")
    blocks = lax.axis_size("blk")
    count, width = features.shape
    share = count // replicas
    rep = lax.axis_index("rep")
    rep_ref = rep.astype(jnp.int32).reshape(1)
    homes = blocks // 2
    order = ring_order(homes)
    after = lax.optimization_barrier

    def ring(x):
        moves = []
        for p in range(homes):
            for c in range(2):
                onward = (p + c) % 2 == 0 if homes % 2 == 0 else c == 0
                core = 1 - c if homes % 2 == 0 else c
                moves.append((order[p] * 2 + c, order[(p + (1 if onward else -1)) % homes] * 2 + core))
        return lax.ppermute(x, "blk", moves)

    def other_core(x):
        return lax.ppermute(x, "blk", [(b, b ^ 1) for b in range(blocks)])

    def scaled(x):
        return jnp.concatenate(scale(x[:, :width], x[:, width:]), axis=1)

    slices = after([lax.dynamic_slice_in_dim(x, rep * share, share) for x in (features, factors)])
    own = jnp.concatenate(slices, axis=1)
    first = ring(own)
    own, features, factors = after((own, features, factors))
    part = share // 2 if replicas <= 2 and share % 32 == 0 else count
    made = own_rows(rep_ref, replicas, features, factors, part)
    filled, parts = made[:2], made[2:]
    own_block = list(zip(parts[::2], parts[1::2], strict=True))
    parts = [other_core(x) for x in parts]
    if part < share:
        beside = [jnp.concatenate(parts[k - 2 * (share // part) :: 2]) for k in (0, 1)]
    else:
        beside = [x[part - share :] for x in parts[-2:]]
    second = ring(jnp.concatenate(beside, axis=1))
    feat, fac = other_rows(share, parts, filled)
    mine_at = 2 * share * (replicas - 1)

    full = (homes - 1) // 2
    total = 2 * full + (homes + 1) % 2
    cut = share // 2 if total > 2 and share % (2 * width) == 0 else 0
    flying, last = [first, second], []
    acc = None
    early = len(own_block) // 2
    mine = pairs(feat, fac, own_block[:early], None, mine_at, 2 * share) if early else None
    for step in range(total - 1):
        here, feat, fac, acc, mine = after((flying[step % 2], feat, fac, acc, mine))
        if step == 0:
            here = scaled(here)
        if step + 2 < total:
            if cut and step + 3 == total:
                last = [ring(here[:cut]), ring(here[cut:])]
            else:
                flying[step % 2] = ring(here)
        if step + 2 < total:
            acc = pairs(feat, fac, [here], acc)
        if step == min(3, total - 2):
            acc, mine = after((acc, mine))
            mine = pairs(feat, fac, own_block[early:], mine, mine_at, 2 * share, mine_at)
    if total < 2:
        mine = pairs(feat, fac, own_block[early:], mine, mine_at, 2 * share, mine_at)
    last = last or [flying[(total - 1) % 2] if total > 1 else scaled(first)]
    late = [here, *last] if total > 1 else last

    def across(by):
        return [
            (b * replicas + r, (b ^ 1) * replicas + (r + by) % replicas) for b in range(blocks) for r in range(replicas)
        ]

    theirs = acc
    for x in late[:-1] if mine_at else []:
        x, theirs = after((x, theirs))
        theirs = pairs(feat, fac, [x], theirs, 0, mine_at)
    end, theirs, acc = after((late[-1], theirs, acc))
    late = [*late[:-1], end]
    arrived = []
    for k in range(replicas - 1):
        at = k * 2 * share
        received = other_core(pairs(feat, fac, [end], theirs, at + share, share))
        part = pairs(feat, fac, [end], theirs, at, share) + received
        arrived.append(lax.ppermute(part, ("blk", "rep"), across(k + 1)))
        acc, part = after((acc, part))
    part = pairs(feat, fac, late, acc, mine_at, 2 * share, 0, mine)
    half = share // 2
    part = part[share:] + jnp.concatenate([other_core(part[:half]), other_core(part[half:share])])
    for x in arrived:
        part = part + x
    return part * (1.0 / (width * math.sqrt(math.log2(math.e) / width)))


def solution(mesh):
    placed = (P("blk", None), P("blk", None))
    return jax.shard_map(
        body, mesh=mesh, in_specs=placed, out_specs=P(("blk", "rep"), None), check_vma=False
    )
```
